256 devices in a mesh: sf: 128 (over x, z, y), wa: 2 (over core).
Axes of the slice: x: 4, y: 4, z: 8, core: 2. Of those that a mesh axis runs over, the one named last changes fastest.
Arguments:
- visibilities: bfloat16 [2, 128, 2, 8, 128], P(None, 'sf', 'wa'), may hold values from -6 to 6
- kernels: bfloat16 [2, 8, 128, 2, 8, 128], P(None, None, 'sf', 'wa'), may hold values from 0.19921875 to 1.1953125
- vis_offsets: int32 [2, 128, 2, 8, 128], P(None, 'sf', 'wa'), may hold values from 0 to 504
- block_counts: int32 [128, 2], P('sf', 'wa'), may hold values from 1 to 8, as said below
- sub_rows: int32 [16], replicated, may hold values from 0 to 448, as said below
- sub_cols: int32 [8], replicated, may hold values from 0 to 448, as said below
- facet_rows: int32 [16], replicated, may hold values from 0 to 448, as said below
- facet_cols: int32 [8], replicated, may hold values from 0 to 448, as said below
- screen_n: float32 [128, 512, 512], P('sf'), may hold values from 0 to 1
- layer_w: float32 [2], replicated, may hold values from 0.5 to 2
Outputs:
- image: float32 [2, 128, 512, 512], P(None, 'sf', 'wa')
The draws below stay inside these ranges and needn't reach their ends.
Inputs may be any that keep to these rules, and one draw needn't show every extreme that they name: `block_counts`: live blocks of one subgrid and layer; some subgrid and layer has all 8 slots live. `sub_rows`: distinct values; one of them is the most. `sub_cols`: distinct values; one of them is the most. `facet_rows`: distinct values; one of them is the most. `facet_cols`: distinct values; one of them is the most.
All inputs are finite; a program needn't handle non-finite values.
Results may differ from the reference program's by a relative error of at most 0.0099.
Values may be sent and summed in bfloat16 or wider, within the bound.
No kernel may reach another device: no remote copies, remote signals or barrier semaphores. Data moves between devices by JAX's collectives and lax.ppermute only.
A program may use at most 64 MiB of HBM per device.

```python
import math
from functools import partial
import jax
import jax.numpy as jnp
from jax import lax

SUB = 512
CON = 64
FAC = 512
SUPP = 8
VB = 128
BLK_CAP = 8
SUB_COLS = 8
FAC_COLS = 8
SUBGRIDS = 128
SUB_ROWS = 16
FACETS = 128
FAC_ROWS = 16
LAYERS = 2


def draw_block_counts(key, part):
    shifts = jax.random.randint(jax.random.fold_in(key, 11), (SUBGRIDS, LAYERS), 0, 4)
    counts = jnp.maximum(BLK_CAP // jnp.left_shift(jnp.ones_like(shifts), shifts), 1)
    chosen = jax.random.randint(jax.random.fold_in(key, 12), (), 0, SUBGRIDS * LAYERS)
    counts = counts.reshape(-1).at[chosen].set(BLK_CAP).reshape(SUBGRIDS, LAYERS)
    return counts.astype(jnp.int32)


def distinct_offsets(key, count, span):
    shuffled = jax.random.permutation(jax.random.fold_in(key, 1), jnp.arange(span - 1, dtype=jnp.int32))
    picked = shuffled[:count].astype(jnp.int32)
    position = jax.random.randint(jax.random.fold_in(key, 2), (), 0, count)
    return picked.at[position].set(span - 1).astype(jnp.int32)


def draw_sub_rows(key, part):
    key = jax.random.fold_in(key, 21)
    return distinct_offsets(key, SUB_ROWS, FAC - CON + 1)


def draw_sub_cols(key, part):
    key = jax.random.fold_in(key, 22)
    return distinct_offsets(key, SUB_COLS, FAC - CON + 1)


def draw_facet_rows(key, part):
    key = jax.random.fold_in(key, 23)
    return distinct_offsets(key, FAC_ROWS, SUB - CON + 1)


def draw_facet_cols(key, part):
    key = jax.random.fold_in(key, 24)
    return distinct_offsets(key, FAC_COLS, SUB - CON + 1)


def place_ends(drawn, stream_key, least, largest):
    dims = drawn.shape
    spot = [jax.random.randint(jax.random.fold_in(stream_key, axis), (), 0, dims[axis]) for axis in range(len(dims))]
    drawn = drawn.at[tuple(spot)].set(least)
    longest = dims.index(max(dims))
    spot[longest] = (spot[longest] + 1) % dims[longest]
    return drawn.at[tuple(spot)].set(largest)


def steps_of(rng, dims, cuts, low, high):
    factor_of, own = 1.0, jax.random.fold_in(rng, 6)
    for dim, blocks in cuts:
        draws = jnp.exp(jax.random.uniform(jax.random.fold_in(own, dim), (blocks,), jnp.float32, low / len(cuts), high / len(cuts)))
        factor_of = factor_of * jnp.repeat(draws, dims[dim] // blocks).reshape([-1 if axis == dim else 1 for axis in range(len(dims))])
    return factor_of


def centred(own_key, shape, scale, most, cuts=(), held_as=jnp.bfloat16):
    level = steps_of(own_key, shape, cuts, -0.22, 0.18) if cuts else 1.0
    entries = jax.random.normal(own_key, shape, jnp.float32) * scale * level
    return jnp.minimum(jnp.maximum(entries, -most), most).astype(held_as)


def setup_inputs(seed: int = 0) -> dict:
    arg_keys = jax.random.split(jax.random.key(seed), 11)
    return {
        "visibilities": centred(arg_keys[0], (2, SUBGRIDS, LAYERS, BLK_CAP, VB), 1.0, 6.0, ((1, 128), (2, 2))),
        "kernels": jnp.clip(0.19921875 + 0.99609375 * jax.random.uniform(arg_keys[1], (2, SUPP, SUBGRIDS, LAYERS, BLK_CAP, VB), jnp.float32) ** steps_of(arg_keys[1], (2, SUPP, SUBGRIDS, LAYERS, BLK_CAP, VB), ((2, 128), (3, 2)), -0.2, 0.2), 0.19921875, 1.1953125).astype(jnp.bfloat16),
        "vis_offsets": place_ends(jax.random.randint(arg_keys[2], (2, SUBGRIDS, LAYERS, BLK_CAP, VB), 0, SUB - SUPP + 1), jax.random.fold_in(arg_keys[2], 1), 0, SUB - SUPP).astype(jnp.int32),
        "block_counts": draw_block_counts(jax.random.fold_in(arg_keys[10], 71), 0),
        "sub_rows": draw_sub_rows(jax.random.fold_in(arg_keys[10], 71), 0),
        "sub_cols": draw_sub_cols(jax.random.fold_in(arg_keys[10], 71), 0),
        "facet_rows": draw_facet_rows(jax.random.fold_in(arg_keys[10], 71), 0),
        "facet_cols": draw_facet_cols(jax.random.fold_in(arg_keys[10], 71), 0),
        "screen_n": jnp.clip(1.0 * jax.random.uniform(arg_keys[8], (FACETS, FAC, FAC), jnp.float32) ** steps_of(arg_keys[8], (FACETS, FAC, FAC), ((0, 128),), -0.2, 0.2), 0.0, 1.0),
        "layer_w": jnp.clip(jax.random.uniform(arg_keys[9], (LAYERS,), jnp.float32, 0.5, 2.0), 0.5, 2.0),
    }


TWO_PI = 2.0 * math.pi

def phase_table(offsets, extent, period, direction):
    frequency = (offsets[:, None] + lax.broadcasted_iota(jnp.int32, (offsets.shape[0], extent), 1)).reshape(-1)
    cell_index = lax.broadcasted_iota(jnp.int32, (frequency.shape[0], period), 1)
    wrapped = frequency[:, None] * cell_index % period
    phases = direction * TWO_PI / period * wrapped.astype(jnp.float32)
    norm_scale = 1.0 / math.sqrt(period)
    return ((jnp.cos(phases) * norm_scale).astype(jnp.bfloat16), (jnp.sin(phases) * norm_scale).astype(jnp.bfloat16))

def complex_dot(first_real, first_imag, second_real, second_imag, numbers):
    product = partial(lax.dot_general, dimension_numbers=numbers, preferred_element_type=jnp.float32)
    return (product(first_real, second_real) - product(first_imag, second_imag), product(first_real, second_imag) + product(first_imag, second_real))

def kernel_rows(kernel_table, offsets, extent):
    cell_shift = lax.broadcasted_iota(jnp.int32, (offsets.shape[0], extent), 1) - offsets[:, None]
    kernel_grid = jnp.zeros((offsets.shape[0], extent), kernel_table.dtype)
    for column in range(kernel_table.shape[0]):
        kernel_grid = jnp.where(cell_shift == column, kernel_table[column][:, None], kernel_grid)
    return kernel_grid

def grid_rows(real_part, imag_part, kernel_values, offsets, extent):
    spread = kernel_rows(kernel_values[0], offsets[0], extent)
    second_grid = kernel_rows(kernel_values[1], offsets[1], extent).astype(jnp.float32)
    weighted_real = (real_part.astype(jnp.float32)[:, None] * second_grid).astype(jnp.bfloat16)
    weighted_imag = (imag_part.astype(jnp.float32)[:, None] * second_grid).astype(jnp.bfloat16)
    weighted = jnp.concatenate([weighted_real, weighted_imag], axis=1)
    return lax.dot_general(spread, weighted, (((0,), (0,)), ((), ())), preferred_element_type=jnp.float32)

def contribute(sub_real, sub_imag, facet_rows, facet_cols):
    period = sub_real.shape[0]
    rows_real, rows_imag = phase_table(facet_rows, CON, period, -1.0)
    cols_real, cols_imag = phase_table(facet_cols, CON, period, -1.0)
    half_real, half_imag = complex_dot(sub_real, sub_imag, cols_real, cols_imag, (((1,), (1,)), ((), ())))
    half_real = half_real.astype(jnp.bfloat16)
    half_imag = half_imag.astype(jnp.bfloat16)
    part_real, part_imag = complex_dot(rows_real, rows_imag, half_real, half_imag, (((1,), (0,)), ((), ())))
    stacked = jnp.stack([part_real, part_imag]).astype(jnp.bfloat16)
    row_count = facet_rows.shape[0]
    col_count = facet_cols.shape[0]
    stacked = stacked.reshape(2, row_count, CON, col_count, CON).transpose(1, 3, 0, 2, 4)
    return stacked.reshape(row_count * col_count, 2 * CON * CON)

def expand(blocks, sub_rows, sub_cols, row_start, row_count):
    row_total = sub_rows.shape[0]
    col_total = sub_cols.shape[0]
    placed = blocks.reshape(row_total, col_total, 2, CON, CON).transpose(2, 0, 3, 1, 4)
    placed = placed.reshape(2, row_total * CON, col_total * CON)
    rows_real, rows_imag = phase_table(sub_rows, CON, FAC, 1.0)
    rows_real = lax.dynamic_slice_in_dim(rows_real, row_start, row_count, 1)
    rows_imag = lax.dynamic_slice_in_dim(rows_imag, row_start, row_count, 1)
    middle_real, middle_imag = complex_dot(rows_real, rows_imag, placed[0], placed[1], (((0,), (0,)), ((), ())))
    middle_real = middle_real.astype(jnp.bfloat16)
    middle_imag = middle_imag.astype(jnp.bfloat16)
    cols_real, cols_imag = phase_table(sub_cols, CON, FAC, 1.0)
    return complex_dot(middle_real, middle_imag, cols_real, cols_imag, (((1,), (0,)), ((), ())))

def screen_term(facet_real, facet_imag, screen, weight):
    phases = TWO_PI * weight * screen
    cosine = jnp.cos(phases)
    sine_part = jnp.sin(phases)
    return jnp.stack([facet_real * cosine - facet_imag * sine_part, facet_real * sine_part + facet_imag * cosine])

def reference(visibilities, kernels, vis_offsets, block_counts, sub_rows, sub_cols, facet_rows, facet_cols, screen_n, layer_w):

    def one_subgrid(subgrid_index):
        source = subgrid_index // LAYERS
        layer_index = subgrid_index % LAYERS
        samples = visibilities[:, source, layer_index].reshape(2, -1)
        kernel_values = kernels[:, :, source, layer_index].reshape(2, SUPP, -1)
        offsets = vis_offsets[:, source, layer_index].reshape(2, -1)
        live_count = block_counts[source, layer_index]
        live_mask = lax.broadcasted_iota(jnp.int32, (BLK_CAP * VB,), 0) // VB < live_count
        samples = jnp.where(live_mask[None, :], samples, jnp.zeros_like(samples))
        gridded = grid_rows(samples[0], samples[1], kernel_values, offsets, SUB).astype(jnp.bfloat16)
        return contribute(gridded[:, :SUB], gridded[:, SUB:], facet_rows, facet_cols)
    pieces = lax.map(one_subgrid, jnp.arange(SUBGRIDS * LAYERS, dtype=jnp.int32))
    pieces = pieces.reshape(SUBGRIDS, LAYERS, FACETS, 2 * CON * CON)

    def one_facet(facet_index):
        facet_image = jnp.zeros((2, FAC, FAC), jnp.float32)
        for layer_index in range(LAYERS):
            blocks = pieces[:, layer_index, facet_index]
            facet_real, facet_imag = expand(blocks, sub_rows, sub_cols, 0, FAC)
            facet_image = facet_image + screen_term(facet_real, facet_imag, screen_n[facet_index], layer_w[layer_index])
        return facet_image
    images = lax.map(one_facet, jnp.arange(FACETS, dtype=jnp.int32))
    return images.transpose(1, 0, 2, 3)
```

```python
import math

import jax
import jax.numpy as jnp
from jax import lax
from jax.experimental import pallas as pl
from jax.experimental.pallas import tpu as pltpu
from jax.sharding import PartitionSpec as P

SUB = 512
CON = 64
FAC = 512
VB = 128
F32 = jnp.float32
BF16 = jnp.bfloat16
NORM = 1.0 / math.sqrt(512.0)
NN = (((1,), (0,)), ((), ()))
NT = (((1,), (1,)), ((), ()))


def dot(first, second, numbers=NN):
    return lax.dot_general(first, second, numbers, preferred_element_type=F32)


def iota(shape, axis):
    return lax.broadcasted_iota(jnp.int32, shape, axis)


def sincos_small(theta):
    square = theta * theta
    cosine = 1.0 + square * (-0.5 + square * (1.0 / 24 + square * (-1.0 / 720 + square * (1.0 / 40320))))
    sine = theta * (1.0 + square * (-1.0 / 6 + square * (1.0 / 120 + square * (-1.0 / 5040 + square * (1.0 / 362880)))))
    return cosine, sine


def rotate_quarter(cosine, sine, quarter):
    odd = (quarter & 1) == 1
    real = jnp.where(odd, sine, cosine)
    imag = jnp.where(odd, cosine, sine)
    real = jnp.where(((quarter + 1) & 2) == 2, -real, real)
    imag = jnp.where((quarter & 2) == 2, -imag, imag)
    return real, imag


def unit_roots(steps):
    quarter = (steps + 64) >> 7
    rest = steps - (quarter << 7)
    cosine, sine = sincos_small(rest.astype(F32) * (2.0 * math.pi / 512))
    return rotate_quarter(cosine, sine, quarter)


def times(first, second):
    return (
        first[0] * second[0] - first[1] * second[1],
        first[0] * second[1] + first[1] * second[0],
    )


def cell_roots():
    low = unit_roots(iota((8, 512), 0) * iota((8, 512), 1) & 511)
    high = unit_roots(iota((8, 512), 0) * 8 * iota((8, 512), 1) & 511)
    real, imag = [], []
    for index in range(8):
        row = slice(index, index + 1)
        product = times((high[0][row], high[1][row]), low)
        real.append(product[0])
        imag.append(product[1])
    return jnp.concatenate(real, axis=0), jnp.concatenate(imag, axis=0)


def offset_roots(offsets_ref, count, lead=None):
    rows = iota((count, 512), 0)
    start = jnp.zeros((count, 512), jnp.int32)
    for index in range(count):
        start = jnp.where(rows == index, offsets_ref[index], start)
    steps = start * iota((count, 512), 1)
    real, imag = unit_roots(steps & 511)
    return real * NORM, imag * NORM


def lane_steps(offsets_ref, count, width):
    shape = (8, count * width)
    lane = iota(shape, 1)
    owner = lane // width
    start = jnp.zeros(shape, jnp.int32)
    for index in range(count):
        start = jnp.where(owner == index, offsets_ref[index], start)
    return start + (lane & 63), lane


def lane_roots(frequency, lead):
    row = iota(frequency.shape, 0)
    high = unit_roots((frequency * row * 64) & 511)
    middle = unit_roots((frequency * row * 8) & 511)
    low = unit_roots((frequency * row + lead) & 511)
    low = (low[0] * NORM, low[1] * NORM)
    return high, middle, low


def row_pick(pair, index):
    return pair[0][index : index + 1], pair[1][index : index + 1]


def front_kernel(
    counts_ref, rows_ref, cols_ref, vis_ref, kernels_ref, offsets_ref, out_ref,
    spread, weighted, col_table, row_small, cell, stacked, row_table,
):
    @pl.when(pl.program_id(0) == 0)
    def _():
        slot = iota((8, 128), 0)
        live = counts_ref[0, 0]
        vis = vis_ref[...].astype(F32)
        tile = iota((64, 8, 128), 0)
        for block in range(8):
            lanes = slice(block * VB, (block + 1) * VB)
            rolled, home = [], []
            for axis in range(2):
                shift = slot - offsets_ref[axis, block : block + 1, :]
                values = jnp.zeros((8, VB), F32)
                for column in range(8):
                    entry = kernels_ref[axis, column, block : block + 1, :].astype(F32)
                    values = jnp.where((shift & 7) == column, entry, values)
                rolled.append(values)
                home.append(-(shift >> 3))
            here = tile == home[0][None]
            spread[:, lanes] = jnp.where(here, rolled[0][None], 0.0).reshape(512, VB).astype(BF16)
            here = tile == home[1][None]
            for part in range(2):
                sample = jnp.where(block < live, vis[part, block : block + 1, :], 0.0)
                value = rolled[1] * sample
                weighted[part * 512 : (part + 1) * 512, lanes] = (
                    jnp.where(here, value[None], 0.0).reshape(512, VB).astype(BF16)
                )
        frequency, lane = lane_steps(cols_ref, 8, 128)
        high, middle, low = lane_roots(frequency, jnp.where((lane & 64) == 0, 0, 128))
        for index in range(8):
            outer = row_pick(high, index)
            for inner in range(8):
                real, imag = times(times(outer, row_pick(middle, inner)), low)
                base = index * 64 + inner * 8
                col_table[base : base + 8, :] = real
                col_table[512 + base : 512 + base + 8, :] = imag
        subgrid = dot(spread[...], weighted[...], NT).astype(BF16)
        half = dot(subgrid, col_table[...].astype(BF16))
        stacked[:512, :] = half.astype(BF16)
        sign = jnp.where((iota((1, 128), 1) & 64) == 0, -1.0, 1.0)
        for block in range(8):
            lanes = slice(block * 128, (block + 1) * 128)
            stacked[512:, lanes] = (pltpu.roll(half[:, lanes], 64, 1) * sign).astype(BF16)
        small = offset_roots(rows_ref, 16)
        row_small[0] = small[0]
        row_small[1] = small[1]
        base = cell_roots()
        cell[0] = base[0]
        cell[1] = base[1]

    step = pl.program_id(0)
    base = (cell[0], cell[1])
    for local in range(4):
        row = pl.ds(step * 4 + local, 1)
        real, imag = times((row_small[0, row, :], row_small[1, row, :]), base)
        rows = slice(local * 64, (local + 1) * 64)
        row_table[rows, :512] = real.astype(BF16)
        row_table[rows, 512:] = (-imag).astype(BF16)
    result = dot(row_table[...], stacked[...]).astype(BF16)
    for local in range(4):
        for column in range(8):
            out_ref[local * 8 + column] = result[
                local * 64 : (local + 1) * 64, column * 128 : (column + 1) * 128
            ]


def smem():
    return pl.BlockSpec(memory_space=pltpu.SMEM)


def vmem():
    return pl.BlockSpec(memory_space=pltpu.VMEM)


def front(counts, facet_rows, facet_cols, vis, kernels, offsets):
    return pl.pallas_call(
        front_kernel,
        grid=(4,),
        out_shape=jax.ShapeDtypeStruct((128, 64, 128), BF16),
        in_specs=[smem(), smem(), smem(), vmem(), vmem(), vmem()],
        out_specs=pl.BlockSpec((32, 64, 128), lambda i: (i, 0, 0)),
        scratch_shapes=[
            pltpu.VMEM((512, 1024), BF16),
            pltpu.VMEM((1024, 1024), BF16),
            pltpu.VMEM((1024, 1024), F32),
            pltpu.VMEM((2, 16, 512), F32),
            pltpu.VMEM((2, 64, 512), F32),
            pltpu.VMEM((1024, 1024), BF16),
            pltpu.VMEM((256, 1024), BF16),
        ],
        compiler_params=pltpu.CompilerParams(vmem_limit_bytes=40 << 20),
        cost_estimate=pl.CostEstimate(flops=6 * 10**9, bytes_accessed=4 << 20, transcendentals=0),
        name="front",
    )(counts, facet_rows, facet_cols, vis, kernels, offsets)


def tables_kernel(rows_ref, cols_ref, weight_ref, screen_ref, row_out, col_out, screen_out):
    frequency, lane = lane_steps(rows_ref, 16, 64)
    high, middle, low = lane_roots(frequency, 0)
    for index in range(8):
        outer = row_pick(high, index)
        for inner in range(0, 8, 2):
            first = times(times(outer, row_pick(middle, inner)), low)
            second = times(times(outer, row_pick(middle, inner + 1)), low)
            base = index * 64 + inner * 8
            for part in range(2):
                row_out[base : base + 16, part * 1024 : (part + 1) * 1024] = jnp.concatenate(
                    [first[part], second[part]], axis=0
                ).astype(BF16)
    small = offset_roots(cols_ref, 8)
    base = cell_roots()
    for column in range(8):
        real, imag = times(row_pick(small, column), base)
        real, imag = real.astype(BF16), imag.astype(BF16)
        rows = slice(column * 128, column * 128 + 64)
        col_out[rows, :512] = real
        col_out[rows, 512:] = imag
        rows = slice(column * 128 + 64, column * 128 + 128)
        col_out[rows, :512] = -imag
        col_out[rows, 512:] = real
    weight = weight_ref[0] * 4.0
    for chunk in range(8):
        rows = slice(chunk * 64, (chunk + 1) * 64)
        turns = screen_ref[0, rows, :] * weight
        whole = jnp.floor(turns + 0.5)
        cosine, sine = sincos_small((turns - whole) * (0.5 * math.pi))
        real, imag = rotate_quarter(cosine, sine, whole.astype(jnp.int32))
        screen_out[0, rows, :] = real
        screen_out[1, rows, :] = imag


def tables(sub_rows, sub_cols, weight, screen):
    return pl.pallas_call(
        tables_kernel,
        out_shape=[
            jax.ShapeDtypeStruct((512, 2048), BF16),
            jax.ShapeDtypeStruct((1024, 1024), BF16),
            jax.ShapeDtypeStruct((2, 512, 512), F32),
        ],
        in_specs=[smem(), smem(), smem(), vmem()],
        out_specs=[vmem(), vmem(), vmem()],
        compiler_params=pltpu.CompilerParams(vmem_limit_bytes=40 << 20),
        cost_estimate=pl.CostEstimate(flops=10**9, bytes_accessed=16 << 20, transcendentals=0),
        name="tables",
    )(sub_rows, sub_cols, weight, screen)


def facet_half(blocks_ref, row_ref, col_ref, screen_ref, middle):
    sign = jnp.where((iota((1, 128), 1) & 64) == 0, -1.0, 1.0)
    for pair in range(4):
        placed = jnp.concatenate(
            [blocks_ref[:, 2 * pair + part].reshape(1024, 128) for part in range(2)], axis=1
        )
        straight = dot(row_ref[:, :1024], placed)
        crossed = dot(row_ref[:, 1024:], placed)
        for part in range(2):
            lanes = slice(part * 128, part * 128 + 128)
            middle[:, pair * 256 + part * 128 : pair * 256 + part * 128 + 128] = (
                straight[:, lanes] + pltpu.roll(crossed[:, lanes], 64, 1) * sign
            ).astype(BF16)
    facet = dot(middle[...], col_ref[...])
    real, imag = facet[:, :512], facet[:, 512:]
    cosine, sine = screen_ref[0], screen_ref[1]
    return real * cosine - imag * sine, real * sine + imag * cosine


def back_kernel(half_ref, blocks_ref, row_ref, col_ref, screen_ref, out_ref, middle):
    real, imag = facet_half(blocks_ref, row_ref, col_ref, screen_ref, middle)
    out_ref[0] = real.astype(out_ref.dtype)
    out_ref[1] = imag.astype(out_ref.dtype)


def back(half, blocks, row_table, col_table, screen, dtype, name):
    return pl.pallas_call(
        back_kernel,
        grid_spec=pltpu.PrefetchScalarGridSpec(
            num_scalar_prefetch=1,
            grid=(1,),
            in_specs=[
                pl.BlockSpec((16, 8, 64, 128), lambda i, h: (0, 0, 0, 0)),
                pl.BlockSpec((256, 2048), lambda i, h: (h[0], 0)),
                pl.BlockSpec((1024, 1024), lambda i, h: (0, 0)),
                pl.BlockSpec((2, 256, 512), lambda i, h: (0, h[0], 0)),
            ],
            out_specs=pl.BlockSpec((2, 256, 512), lambda i, h: (0, 0, 0)),
            scratch_shapes=[pltpu.VMEM((256, 1024), BF16)],
        ),
        out_shape=jax.ShapeDtypeStruct((2, 256, 512), dtype),
        compiler_params=pltpu.CompilerParams(vmem_limit_bytes=40 << 20),
        cost_estimate=pl.CostEstimate(flops=2 * 10**9, bytes_accessed=8 << 20, transcendentals=0),
        name=name,
    )(half, blocks, row_table, col_table, screen)


def per_device(
    visibilities, kernels, vis_offsets, block_counts,
    sub_rows, sub_cols, facet_rows, facet_cols, screen_n, layer_w,
):
    outgoing = front(
        block_counts, facet_rows, facet_cols,
        visibilities.reshape(2, 8, VB), kernels.reshape(2, 8, 8, VB), vis_offsets.reshape(2, 8, VB),
    )
    incoming = lax.all_to_all(outgoing, "sf", split_axis=0, concat_axis=0, tiled=True)
    layer = lax.axis_index("wa")
    weight = lax.dynamic_slice_in_dim(layer_w, layer, 1)
    row_table, col_table, screen = tables(sub_rows, sub_cols, weight, screen_n)
    blocks = incoming.reshape(16, 8, CON, 128)
    other = (1 - layer).reshape(1)
    sent = back(other, blocks, row_table, col_table, screen, BF16, "back_other")
    received = lax.ppermute(sent, "wa", [(0, 1), (1, 0)])
    own = back(layer.reshape(1), blocks, row_table, col_table, screen, F32, "back_own")
    return (own + received.astype(F32))[:, None]


def solution(mesh):
    in_specs = (
        P(None, "sf", "wa", None, None),
        P(None, None, "sf", "wa", None, None),
        P(None, "sf", "wa", None, None),
        P("sf", "wa"),
        P(),
        P(),
        P(),
        P(),
        P("sf", None, None),
        P(),
    )
    out_specs = P(None, "sf", "wa", None)
    return jax.shard_map(
        per_device, mesh=mesh, in_specs=in_specs, out_specs=out_specs, check_vma=False
    )
```

```python
import math

import jax
import jax.numpy as jnp
from jax import lax
from jax.experimental import pallas as pl
from jax.experimental.pallas import tpu as pltpu
from jax.sharding import PartitionSpec as P

SUB = 512
CON = 64
FAC = 512
VB = 128
F32 = jnp.float32
BF16 = jnp.bfloat16
NORM = 1.0 / math.sqrt(512.0)
NN = (((1,), (0,)), ((), ()))
NT = (((1,), (1,)), ((), ()))


def dot(first, second, numbers=NN):
    return lax.dot_general(first, second, numbers, preferred_element_type=F32)


def iota(shape, axis):
    return lax.broadcasted_iota(jnp.int32, shape, axis)


def sincos_small(theta):
    square = theta * theta
    cosine = 1.0 + square * (-0.5 + square * (1.0 / 24 + square * (-1.0 / 720 + square * (1.0 / 40320))))
    sine = theta * (1.0 + square * (-1.0 / 6 + square * (1.0 / 120 + square * (-1.0 / 5040 + square * (1.0 / 362880)))))
    return cosine, sine


def rotate_quarter(cosine, sine, quarter):
    odd = (quarter & 1) == 1
    real = jnp.where(odd, sine, cosine)
    imag = jnp.where(odd, cosine, sine)
    real = jnp.where(((quarter + 1) & 2) == 2, -real, real)
    imag = jnp.where((quarter & 2) == 2, -imag, imag)
    return real, imag


def unit_roots(steps):
    quarter = (steps + 64) >> 7
    rest = steps - (quarter << 7)
    cosine, sine = sincos_small(rest.astype(F32) * (2.0 * math.pi / 512))
    return rotate_quarter(cosine, sine, quarter)


def times(first, second):
    return (
        first[0] * second[0] - first[1] * second[1],
        first[0] * second[1] + first[1] * second[0],
    )


def cell_roots():
    low = unit_roots(iota((8, 512), 0) * iota((8, 512), 1) & 511)
    high = unit_roots(iota((8, 512), 0) * 8 * iota((8, 512), 1) & 511)
    real, imag = [], []
    for index in range(8):
        row = slice(index, index + 1)
        product = times((high[0][row], high[1][row]), low)
        real.append(product[0])
        imag.append(product[1])
    return jnp.concatenate(real, axis=0), jnp.concatenate(imag, axis=0)


def offset_roots(offsets_ref, count):
    rows = iota((count, 512), 0)
    start = jnp.zeros((count, 512), jnp.int32)
    for index in range(count):
        start = jnp.where(rows == index, offsets_ref[index], start)
    steps = start * iota((count, 512), 1)
    real, imag = unit_roots(steps & 511)
    return real * NORM, imag * NORM


def lane_steps(offsets_ref, count, width):
    shape = (8, count * width)
    lane = iota(shape, 1)
    owner = lane // width
    start = jnp.zeros(shape, jnp.int32)
    for index in range(count):
        start = jnp.where(owner == index, offsets_ref[index], start)
    return start + (lane & 63), lane


def lane_roots(frequency, lead):
    row = iota(frequency.shape, 0)
    high = unit_roots((frequency * row * 64) & 511)
    middle = unit_roots((frequency * row * 8) & 511)
    low = unit_roots((frequency * row + lead) & 511)
    low = (low[0] * NORM, low[1] * NORM)
    return high, middle, low


def row_pick(pair, index):
    return pair[0][index : index + 1], pair[1][index : index + 1]


def pack_kernel(counts_ref, vis_ref, kernels_ref, offsets_ref, out_ref):
    live = counts_ref[0, 0]
    slot = iota((8, 128), 0)
    samples = [jnp.where(slot < live, vis_ref[part].astype(F32), 0.0) for part in range(2)]
    out_ref[0:16, :] = jnp.concatenate(samples, axis=0).astype(BF16)
    for axis in range(2):
        offsets = offsets_ref[axis]
        low = offsets & 7
        digits = jnp.concatenate([(offsets >> 3).astype(F32), low.astype(F32)], axis=0)
        out_ref[16 + axis * 16 : 32 + axis * 16, :] = digits.astype(BF16)
        turned = []
        for block in range(8):
            shift = (slot - low[block : block + 1, :]) & 7
            values = jnp.zeros((8, VB), F32)
            for column in range(8):
                entry = kernels_ref[axis, column, block : block + 1, :].astype(F32)
                values = jnp.where(shift == column, entry, values)
            turned.append(values)
        out_ref[48 + axis * 64 : 112 + axis * 64, :] = jnp.concatenate(turned, axis=0).astype(BF16)


def pack(counts, vis, kernels, offsets):
    return pl.pallas_call(
        pack_kernel,
        out_shape=jax.ShapeDtypeStruct((176, 128), BF16),
        in_specs=[smem(), vmem(), vmem(), vmem()],
        out_specs=vmem(),
        compiler_params=pltpu.CompilerParams(vmem_limit_bytes=4 << 20),
        name="pack",
    )(counts, vis, kernels, offsets)


def lane_table(offsets_ref, count, width, lead, out_ref, place):
    frequency, lane = lane_steps(offsets_ref, count, width)
    high, middle, low = lane_roots(frequency, jnp.where((lane & lead) == 0, 0, 128))
    for index in range(8):
        outer = row_pick(high, index)
        for inner in range(0, 8, 2):
            first = times(times(outer, row_pick(middle, inner)), low)
            second = times(times(outer, row_pick(middle, inner + 1)), low)
            base = index * 64 + inner * 8
            for part in range(2):
                place(out_ref, part, base, jnp.concatenate([first[part], second[part]], axis=0).astype(BF16))


def facet_tables_kernel(group_ref, rows_ref, cols_ref, row_out, col_out):
    def below(ref, part, base, value):
        ref[part * 512 + base : part * 512 + base + 16, :] = value

    lane_table(cols_ref, 8, 128, 64, col_out, below)
    base = cell_roots()
    small = offset_roots([rows_ref[4 * index + group_ref[0]] for index in range(4)], 4)
    for index in range(4):
        real, imag = times(row_pick(small, index), base)
        row_out[index * 64 : index * 64 + 64, :] = real.astype(BF16)
        row_out[256 + index * 64 : 320 + index * 64, :] = (-imag).astype(BF16)


def facet_tables(group, facet_rows, facet_cols):
    return pl.pallas_call(
        facet_tables_kernel,
        out_shape=[
            jax.ShapeDtypeStruct((512, 512), BF16),
            jax.ShapeDtypeStruct((1024, 1024), BF16),
        ],
        in_specs=[smem(), smem(), smem()],
        out_specs=[vmem(), vmem()],
        compiler_params=pltpu.CompilerParams(vmem_limit_bytes=8 << 20),
        cost_estimate=pl.CostEstimate(flops=10**9, bytes_accessed=4 << 20, transcendentals=0),
        name="facet_tables",
    )(group, facet_rows, facet_cols)


def front_kernel(
    group_ref, own_ref, first_ref, second_ref, third_ref, row_ref, col_ref, out_ref,
    packs, spread, second_spread, turned, halves,
):
    step = pl.program_id(0)

    @pl.when(step == 0)
    def _():
        for index, ref in enumerate((own_ref, first_ref, second_ref, third_ref)):
            packs[index] = ref[...]

    slot = iota((8, 128), 0)
    tile = iota((64, 8, 128), 0)
    samples = packs[step, 0:16, :].astype(F32)
    for axis, target in ((0, spread), (1, second_spread)):
        digits = packs[step, 16 + axis * 16 : 32 + axis * 16, :].astype(jnp.int32)
        kernels = packs[step, 48 + axis * 64 : 112 + axis * 64, :].astype(F32)
        for block in range(8):
            home = digits[block : block + 1, :] + (digits[block + 8 : block + 9, :] > slot).astype(jnp.int32)
            values = kernels[block * 8 : block * 8 + 8, :]
            target[:, block * VB : (block + 1) * VB] = (
                jnp.where(tile == home[None], values[None], 0.0).reshape(512, VB).astype(BF16)
            )
    for quarter in range(4):
        lanes = slice(quarter * 256, (quarter + 1) * 256)
        rows = dot(row_ref[...], spread[:, lanes])
        real_part = jnp.concatenate([samples[2 * quarter + part : 2 * quarter + part + 1] for part in range(2)], axis=1)
        imag_part = jnp.concatenate([samples[2 * quarter + part + 8 : 2 * quarter + part + 9] for part in range(2)], axis=1)
        real, imag = times((rows[:256], rows[256:]), (real_part, imag_part))
        turned[:256, lanes] = real.astype(BF16)
        turned[256:, lanes] = imag.astype(BF16)
    half = dot(turned[...], second_spread[...], NT).astype(BF16)
    halves[:, :512] = half[:256]
    halves[:, 512:] = half[256:]
    result = dot(halves[...], col_ref[...]).astype(BF16)
    for row in range(4):
        for column in range(8):
            out_ref[row * 8 + column, 0] = result[row * 64 : (row + 1) * 64, column * 128 : (column + 1) * 128]


def smem():
    return pl.BlockSpec(memory_space=pltpu.SMEM)


def vmem():
    return pl.BlockSpec(memory_space=pltpu.VMEM)


def front(group, packs, row_table, col_table):
    whole = lambda *shape: pl.BlockSpec(shape, lambda i, g: (0,) * len(shape))
    return pl.pallas_call(
        front_kernel,
        grid_spec=pltpu.PrefetchScalarGridSpec(
            num_scalar_prefetch=1,
            grid=(4,),
            in_specs=[whole(176, 128)] * 4 + [whole(512, 512), whole(1024, 1024)],
            out_specs=pl.BlockSpec((32, 1, 64, 128), lambda i, g: (0, (g[0] + 4 - i) & 3, 0, 0)),
            scratch_shapes=[
                pltpu.VMEM((4, 176, 128), BF16),
                pltpu.VMEM((512, 1024), BF16),
                pltpu.VMEM((512, 1024), BF16),
                pltpu.VMEM((512, 1024), BF16),
                pltpu.VMEM((256, 1024), BF16),
            ],
        ),
        out_shape=jax.ShapeDtypeStruct((32, 4, 64, 128), BF16),
        compiler_params=pltpu.CompilerParams(vmem_limit_bytes=20 << 20),
        cost_estimate=pl.CostEstimate(flops=6 * 10**9, bytes_accessed=4 << 20, transcendentals=0),
        name="front",
    )(group, *packs, row_table, col_table)


def tables_kernel(rows_ref, cols_ref, weight_ref, screen_ref, row_out, col_out, screen_out):
    def beside(ref, part, base, value):
        ref[base : base + 16, part * 1024 : (part + 1) * 1024] = value

    lane_table(rows_ref, 16, 64, 0, row_out, beside)
    small = offset_roots(cols_ref, 8)
    base = cell_roots()
    for column in range(8):
        real, imag = times(row_pick(small, column), base)
        real, imag = real.astype(BF16), imag.astype(BF16)
        rows = slice(column * 128, column * 128 + 64)
        col_out[rows, :512] = real
        col_out[rows, 512:] = imag
        rows = slice(column * 128 + 64, column * 128 + 128)
        col_out[rows, :512] = -imag
        col_out[rows, 512:] = real
    weight = weight_ref[0] * 4.0
    for chunk in range(8):
        rows = slice(chunk * 64, (chunk + 1) * 64)
        turns = screen_ref[0, rows, :] * weight
        whole = jnp.floor(turns + 0.5)
        cosine, sine = sincos_small((turns - whole) * (0.5 * math.pi))
        real, imag = rotate_quarter(cosine, sine, whole.astype(jnp.int32))
        screen_out[0, rows, :] = real
        screen_out[1, rows, :] = imag


def tables(sub_rows, sub_cols, weight, screen):
    return pl.pallas_call(
        tables_kernel,
        out_shape=[
            jax.ShapeDtypeStruct((512, 2048), BF16),
            jax.ShapeDtypeStruct((1024, 1024), BF16),
            jax.ShapeDtypeStruct((2, 512, 512), F32),
        ],
        in_specs=[smem(), smem(), smem(), vmem()],
        out_specs=[vmem(), vmem(), vmem()],
        compiler_params=pltpu.CompilerParams(vmem_limit_bytes=20 << 20),
        cost_estimate=pl.CostEstimate(flops=10**9, bytes_accessed=16 << 20, transcendentals=0),
        name="tables",
    )(sub_rows, sub_cols, weight, screen)


def facet_half(blocks_ref, row_ref, col_ref, screen_ref, middle):
    sign = jnp.where((iota((1, 128), 1) & 64) == 0, -1.0, 1.0)
    for pair in range(4):
        placed = jnp.concatenate(
            [blocks_ref[:, 2 * pair + part].reshape(1024, 128) for part in range(2)], axis=1
        )
        straight = dot(row_ref[:, :1024], placed)
        crossed = dot(row_ref[:, 1024:], placed)
        for part in range(2):
            lanes = slice(part * 128, part * 128 + 128)
            middle[:, pair * 256 + part * 128 : pair * 256 + part * 128 + 128] = (
                straight[:, lanes] + pltpu.roll(crossed[:, lanes], 64, 1) * sign
            ).astype(BF16)
    facet = dot(middle[...], col_ref[...])
    real, imag = facet[:, :512], facet[:, 512:]
    cosine, sine = screen_ref[0], screen_ref[1]
    return real * cosine - imag * sine, real * sine + imag * cosine


def back_kernel(half_ref, blocks_ref, row_ref, col_ref, screen_ref, out_ref, middle):
    real, imag = facet_half(blocks_ref, row_ref, col_ref, screen_ref, middle)
    out_ref[0] = real.astype(out_ref.dtype)
    out_ref[1] = imag.astype(out_ref.dtype)


def back(half, blocks, row_table, col_table, screen, dtype, name):
    return pl.pallas_call(
        back_kernel,
        grid_spec=pltpu.PrefetchScalarGridSpec(
            num_scalar_prefetch=1,
            grid=(1,),
            in_specs=[
                pl.BlockSpec((4, 8, 4, 64, 128), lambda i, h: (0, 0, 0, 0, 0)),
                pl.BlockSpec((256, 2048), lambda i, h: (h[0], 0)),
                pl.BlockSpec((1024, 1024), lambda i, h: (0, 0)),
                pl.BlockSpec((2, 256, 512), lambda i, h: (0, h[0], 0)),
            ],
            out_specs=pl.BlockSpec((2, 256, 512), lambda i, h: (0, 0, 0)),
            scratch_shapes=[pltpu.VMEM((256, 1024), BF16)],
        ),
        out_shape=jax.ShapeDtypeStruct((2, 256, 512), dtype),
        compiler_params=pltpu.CompilerParams(vmem_limit_bytes=20 << 20),
        cost_estimate=pl.CostEstimate(flops=2 * 10**9, bytes_accessed=8 << 20, transcendentals=0),
        name=name,
    )(half, blocks, row_table, col_table, screen)


def position(x, z, y):
    return x * 32 + (z % 8) * 4 + y


GROUPS = [
    [position(x, 2 * k + l, y) for x in range(4) for l in range(2) for y in range(4)] for k in range(4)
]


def shifted(turn):
    return [
        (position(x, z, y), position(x, z + 2 * turn, y)) for x in range(4) for z in range(8) for y in range(4)
    ]


def per_device(
    visibilities, kernels, vis_offsets, block_counts,
    sub_rows, sub_cols, facet_rows, facet_cols, screen_n, layer_w,
):
    place = lax.axis_index("sf")
    group = ((place >> 3) & 3).reshape(1)
    own = pack(
        block_counts,
        visibilities.reshape(2, 8, VB), kernels.reshape(2, 8, 8, VB), vis_offsets.reshape(2, 8, VB),
    )
    packs = [own] + [lax.ppermute(own, "sf", shifted(turn)) for turn in (1, 2, 3)]
    facet_row_table, facet_col_table = facet_tables(group, facet_rows, facet_cols)
    outgoing = front(group, packs, facet_row_table, facet_col_table)
    incoming = lax.all_to_all(
        outgoing, "sf", split_axis=0, concat_axis=0, tiled=True, axis_index_groups=GROUPS
    )
    layer = lax.axis_index("wa")
    weight = lax.dynamic_slice_in_dim(layer_w, layer, 1)
    row_table, col_table, screen = tables(sub_rows, sub_cols, weight, screen_n)
    blocks = incoming.reshape(4, 8, 4, CON, 128)
    other = (1 - layer).reshape(1)
    sent = back(other, blocks, row_table, col_table, screen, BF16, "back_other")
    received = lax.ppermute(sent, "wa", [(0, 1), (1, 0)])
    own = back(layer.reshape(1), blocks, row_table, col_table, screen, F32, "back_own")
    return (own + received.astype(F32))[:, None]


def solution(mesh):
    in_specs = (
        P(None, "sf", "wa", None, None),
        P(None, None, "sf", "wa", None, None),
        P(None, "sf", "wa", None, None),
        P("sf", "wa"),
        P(),
        P(),
        P(),
        P(),
        P("sf", None, None),
        P(),
    )
    out_specs = P(None, "sf", "wa", None)
    return jax.shard_map(
        per_device, mesh=mesh, in_specs=in_specs, out_specs=out_specs, check_vma=False
    )
```

```python
import math

import jax
import jax.numpy as jnp
from jax import lax
from jax.experimental import pallas as pl
from jax.experimental.pallas import tpu as pltpu
from jax.sharding import PartitionSpec as P

SUB = 512
CON = 64
FAC = 512
VB = 128
F32 = jnp.float32
BF16 = jnp.bfloat16
NORM = 1.0 / math.sqrt(512.0)
NN = (((1,), (0,)), ((), ()))
NT = (((1,), (1,)), ((), ()))
LIMIT = 64 << 20


def dot(first, second, numbers=NN):
    return lax.dot_general(first, second, numbers, preferred_element_type=F32)


def iota(shape, axis):
    return lax.broadcasted_iota(jnp.int32, shape, axis)


def sincos_small(theta):
    square = theta * theta
    cosine = 1.0 + square * (-0.5 + square * (1.0 / 24 + square * (-1.0 / 720 + square * (1.0 / 40320))))
    sine = theta * (1.0 + square * (-1.0 / 6 + square * (1.0 / 120 + square * (-1.0 / 5040 + square * (1.0 / 362880)))))
    return cosine, sine


def rotate_quarter(cosine, sine, quarter):
    odd = (quarter & 1) == 1
    real = jnp.where(odd, sine, cosine)
    imag = jnp.where(odd, cosine, sine)
    real = jnp.where(((quarter + 1) & 2) == 2, -real, real)
    imag = jnp.where((quarter & 2) == 2, -imag, imag)
    return real, imag


def unit_roots(steps):
    quarter = (steps + 64) >> 7
    rest = steps - (quarter << 7)
    cosine, sine = sincos_small(rest.astype(F32) * (2.0 * math.pi / 512))
    return rotate_quarter(cosine, sine, quarter)


def times(first, second):
    return (
        first[0] * second[0] - first[1] * second[1],
        first[0] * second[1] + first[1] * second[0],
    )


def cell_roots():
    low = unit_roots(iota((8, 512), 0) * iota((8, 512), 1) & 511)
    high = unit_roots(iota((8, 512), 0) * 8 * iota((8, 512), 1) & 511)
    real, imag = [], []
    for index in range(8):
        row = slice(index, index + 1)
        product = times((high[0][row], high[1][row]), low)
        real.append(product[0])
        imag.append(product[1])
    return jnp.concatenate(real, axis=0), jnp.concatenate(imag, axis=0)


def offset_roots(offsets_ref, count):
    rows = iota((count, 512), 0)
    start = jnp.zeros((count, 512), jnp.int32)
    for index in range(count):
        start = jnp.where(rows == index, offsets_ref[index], start)
    steps = start * iota((count, 512), 1)
    real, imag = unit_roots(steps & 511)
    return real * NORM, imag * NORM


def lane_steps(offsets_ref, count, width):
    shape = (8, count * width)
    lane = iota(shape, 1)
    owner = lane // width
    start = jnp.zeros(shape, jnp.int32)
    for index in range(count):
        start = jnp.where(owner == index, offsets_ref[index], start)
    return start + (lane & 63), lane


def lane_roots(frequency, lead):
    row = iota(frequency.shape, 0)
    high = unit_roots((frequency * row * 64) & 511)
    middle = unit_roots((frequency * row * 8) & 511)
    low = unit_roots((frequency * row + lead) & 511)
    low = (low[0] * NORM, low[1] * NORM)
    return high, middle, low


def row_pick(pair, index):
    return pair[0][index : index + 1], pair[1][index : index + 1]


def fetch(sources, targets, sems):
    copies = [
        pltpu.make_async_copy(source, target, sems.at[index])
        for index, (source, target) in enumerate(zip(sources, targets))
    ]
    for copy in copies:
        copy.start()
    return copies


def pack_kernel(counts_hbm, vis_hbm, kernels_hbm, offsets_hbm, out_ref, counts, vis, kernels, all_offsets, sems):
    copies = fetch((counts_hbm, vis_hbm, kernels_hbm, offsets_hbm), (counts, vis, kernels, all_offsets), sems)
    for copy in copies:
        copy.wait()
    live = counts[0, 0]
    slot = iota((8, 128), 0)
    samples = [jnp.where(slot < live, vis[part].astype(F32), 0.0) for part in range(2)]
    out_ref[0:16, :] = jnp.concatenate(samples, axis=0).astype(BF16)
    for axis in range(2):
        offsets = all_offsets[axis]
        low = offsets & 7
        digits = jnp.concatenate([(offsets >> 3).astype(F32), low.astype(F32)], axis=0)
        out_ref[16 + axis * 16 : 32 + axis * 16, :] = digits.astype(BF16)
        turned = []
        for block in range(8):
            shift = (slot - low[block : block + 1, :]) & 7
            values = jnp.zeros((8, VB), F32)
            for column in range(8):
                entry = kernels[axis, column, block : block + 1, :].astype(F32)
                values = jnp.where(shift == column, entry, values)
            turned.append(values)
        out_ref[48 + axis * 64 : 112 + axis * 64, :] = jnp.concatenate(turned, axis=0).astype(BF16)


def pack(counts, vis, kernels, offsets):
    return pl.pallas_call(
        pack_kernel,
        out_shape=jax.ShapeDtypeStruct((176, 128), BF16),
        in_specs=[hbm()] * 4,
        out_specs=vmem(),
        scratch_shapes=[
            pltpu.SMEM((1, 1), jnp.int32),
            pltpu.VMEM((2, 8, VB), BF16),
            pltpu.VMEM((2, 8, 8, VB), BF16),
            pltpu.VMEM((2, 8, VB), jnp.int32),
            pltpu.SemaphoreType.DMA((4,)),
        ],
        compiler_params=pltpu.CompilerParams(vmem_limit_bytes=LIMIT),
        name="pack",
    )(counts, vis, kernels, offsets)


def lane_table(offsets_ref, count, width, lead, out_ref, place):
    frequency, lane = lane_steps(offsets_ref, count, width)
    high, middle, low = lane_roots(frequency, jnp.where((lane & lead) == 0, 0, 128))
    for index in range(8):
        outer = row_pick(high, index)
        for inner in range(0, 8, 2):
            first = times(times(outer, row_pick(middle, inner)), low)
            second = times(times(outer, row_pick(middle, inner + 1)), low)
            base = index * 64 + inner * 8
            for part in range(2):
                place(out_ref, part, base, jnp.concatenate([first[part], second[part]], axis=0).astype(BF16))


def grid_slot(samples, digits, kernels, row_table, col_table, spreads, turned, halves, sent, arrive=None):
    slot = iota((8, 128), 0)
    tile = iota((64, 8, 128), 0)
    for axis in range(2):
        for block in range(8):
            home = digits[axis][block : block + 1, :] + (digits[axis][block + 8 : block + 9, :] > slot).astype(jnp.int32)
            values = kernels[axis][block * 8 : block * 8 + 8, :]
            spreads[axis, :, block * VB : (block + 1) * VB] = (
                jnp.where(tile == home[None], values[None], 0.0).reshape(512, VB).astype(BF16)
            )
    if arrive is not None:
        arrive()
    for quarter in range(4):
        lanes = slice(quarter * 256, (quarter + 1) * 256)
        rows = dot(row_table[...], spreads[0, :, lanes])
        real_part, imag_part = (
            jnp.concatenate([samples[8 * half + 2 * quarter + part : 8 * half + 2 * quarter + part + 1] for part in range(2)], axis=1)
            for half in range(2)
        )
        real, imag = times((rows[:256], rows[256:]), (real_part, imag_part))
        turned[:256, lanes] = real.astype(BF16)
        turned[256:, lanes] = imag.astype(BF16)
    half = dot(turned[...], spreads[1], NT).astype(BF16)
    halves[:, :512] = half[:256]
    halves[:, 512:] = half[256:]
    result = dot(halves[...], col_table[...]).astype(BF16)
    for row in range(4):
        for column in range(8):
            sent[row * 8 + column] = result[row * 64 : (row + 1) * 64, column * 128 : (column + 1) * 128]


def unpacked(ref):
    return (
        ref[0:16, :].astype(F32),
        [ref[16 + axis * 16 : 32 + axis * 16, :].astype(jnp.int32) for axis in range(2)],
        [ref[48 + axis * 64 : 112 + axis * 64, :].astype(F32) for axis in range(2)],
    )


def front_scratch(slots):
    return [
        pltpu.VMEM((2, 512, 1024), BF16),
        pltpu.VMEM((512, 1024), BF16),
        pltpu.VMEM((256, 1024), BF16),
        pltpu.VMEM((slots, 32, 64, 128), BF16),
        pltpu.SemaphoreType.DMA((slots,)),
    ]


def table_scratch():
    return [pltpu.VMEM((512, 512), BF16), pltpu.VMEM((1024, 1024), BF16), pltpu.SemaphoreType.DMA((2,))]


def front_own_kernel(
    group_ref, rows_ref, cols_ref, own_ref, row_hbm, col_hbm, out_hbm,
    spreads, turned, halves, sent, sems, row_out, col_out, table_sems,
):
    def below(ref, part, base, value):
        ref[part * 512 + base : part * 512 + base + 16, :] = value

    lane_table(cols_ref, 8, 128, 64, col_out, below)
    base = cell_roots()
    small = offset_roots([rows_ref[4 * index + group_ref[0]] for index in range(4)], 4)
    for index in range(4):
        real, imag = times(row_pick(small, index), base)
        row_out[index * 64 : index * 64 + 64, :] = real.astype(BF16)
        row_out[256 + index * 64 : 320 + index * 64, :] = (-imag).astype(BF16)
    copies = fetch((row_out, col_out), (row_hbm, col_hbm), table_sems)
    grid_slot(*unpacked(own_ref), row_out, col_out, spreads, turned, halves, sent.at[0])
    copy = pltpu.make_async_copy(sent.at[0], out_hbm.at[:, group_ref[0] & 3], sems.at[0])
    copy.start()
    for copy in copies + [copy]:
        copy.wait()


def front_own(group, facet_rows, facet_cols, own):
    return pl.pallas_call(
        front_own_kernel,
        out_shape=[
            jax.ShapeDtypeStruct((512, 512), BF16),
            jax.ShapeDtypeStruct((1024, 1024), BF16),
            jax.ShapeDtypeStruct((32, 4, 64, 128), BF16),
        ],
        in_specs=[smem(), smem(), smem(), vmem()],
        out_specs=[hbm()] * 3,
        scratch_shapes=front_scratch(1) + table_scratch(),
        compiler_params=pltpu.CompilerParams(vmem_limit_bytes=LIMIT),
        cost_estimate=pl.CostEstimate(flops=3 * 10**9, bytes_accessed=4 << 20, transcendentals=0),
        name="front_own",
    )(group, facet_rows, facet_cols, own)


def front_others_kernel(
    group_ref, first_ref, second_ref, third_ref, row_hbm, col_hbm, begun_hbm, out_hbm,
    spreads, turned, halves, sent, sems, row_table, col_table, table_sems,
):
    tables = fetch((row_hbm, col_hbm), (row_table, col_table), table_sems)

    def arrive():
        for copy in tables:
            copy.wait()

    copies = []
    for index, ref in enumerate((first_ref, second_ref, third_ref)):
        grid_slot(
            *unpacked(ref), row_table, col_table, spreads, turned, halves, sent.at[index],
            arrive if index == 0 else None,
        )
        source = (group_ref[0] + 3 - index) & 3
        copy = pltpu.make_async_copy(sent.at[index], out_hbm.at[:, source], sems.at[index])
        copy.start()
        copies.append(copy)
    for copy in copies:
        copy.wait()


def front_others(group, packs, row_table, col_table, begun):
    return pl.pallas_call(
        front_others_kernel,
        out_shape=jax.ShapeDtypeStruct((32, 4, 64, 128), BF16),
        in_specs=[smem()] + [vmem()] * 3 + [hbm()] * 3,
        out_specs=hbm(),
        scratch_shapes=front_scratch(3) + table_scratch(),
        input_output_aliases={6: 0},
        compiler_params=pltpu.CompilerParams(vmem_limit_bytes=LIMIT),
        cost_estimate=pl.CostEstimate(flops=6 * 10**9, bytes_accessed=4 << 20, transcendentals=0),
        name="front_others",
    )(group, *packs, row_table, col_table, begun)


def smem():
    return pl.BlockSpec(memory_space=pltpu.SMEM)


def vmem():
    return pl.BlockSpec(memory_space=pltpu.VMEM)


def hbm():
    return pl.BlockSpec(memory_space=pltpu.HBM)


def tables_kernel(
    layer_ref, rows_ref, cols_ref, weights_ref, screen_hbm, row_hbm, col_hbm, screen_out_hbm,
    screen, row_out, col_out, screen_out, sems,
):
    layer = layer_ref[0]
    (arrival,) = fetch((screen_hbm.at[0, pl.ds(layer * 256, 256)],), (screen,), sems.at[pl.ds(3, 1)])

    def beside(ref, part, base, value):
        ref[base : base + 16, part * 1024 : (part + 1) * 1024] = value

    lane_table(rows_ref, 16, 64, 0, row_out, beside)
    small = offset_roots(cols_ref, 8)
    base = cell_roots()
    for column in range(8):
        real, imag = times(row_pick(small, column), base)
        real, imag = real.astype(BF16), imag.astype(BF16)
        rows = slice(column * 128, column * 128 + 64)
        col_out[rows, :512] = real
        col_out[rows, 512:] = imag
        rows = slice(column * 128 + 64, column * 128 + 128)
        col_out[rows, :512] = -imag
        col_out[rows, 512:] = real
    arrival.wait()
    for side in range(2):
        weight = weights_ref[layer if side == 0 else 1 - layer] * 4.0
        for chunk in range(4):
            rows = slice(chunk * 64, (chunk + 1) * 64)
            turns = screen[rows, :] * weight
            whole = jnp.floor(turns + 0.5)
            cosine, sine = sincos_small((turns - whole) * (0.5 * math.pi))
            real, imag = rotate_quarter(cosine, sine, whole.astype(jnp.int32))
            screen_out[side, 0, rows, :] = real
            screen_out[side, 1, rows, :] = imag
    for copy in fetch((row_out, col_out, screen_out), (row_hbm, col_hbm, screen_out_hbm), sems):
        copy.wait()


def tables(layer, sub_rows, sub_cols, weights, screen):
    return pl.pallas_call(
        tables_kernel,
        out_shape=[
            jax.ShapeDtypeStruct((512, 2048), BF16),
            jax.ShapeDtypeStruct((1024, 1024), BF16),
            jax.ShapeDtypeStruct((2, 2, 256, 512), F32),
        ],
        in_specs=[smem(), smem(), smem(), smem(), hbm()],
        out_specs=[hbm()] * 3,
        scratch_shapes=[
            pltpu.VMEM((256, 512), F32),
            pltpu.VMEM((512, 2048), BF16),
            pltpu.VMEM((1024, 1024), BF16),
            pltpu.VMEM((2, 2, 256, 512), F32),
            pltpu.SemaphoreType.DMA((4,)),
        ],
        compiler_params=pltpu.CompilerParams(vmem_limit_bytes=LIMIT),
        cost_estimate=pl.CostEstimate(flops=10**9, bytes_accessed=16 << 20, transcendentals=0),
        name="tables",
    )(layer, sub_rows, sub_cols, weights, screen)


def block_copies(blocks_hbm, blocks, sems):
    return fetch(
        [blocks_hbm.at[:, 2 * pair : 2 * pair + 2] for pair in range(4)],
        [blocks.at[:, 2 * pair : 2 * pair + 2] for pair in range(4)],
        sems,
    )


def middle_rows(blocks, copies, row_table, store):
    sign = jnp.where((iota((1, 128), 1) & 64) == 0, -1.0, 1.0)
    for pair in range(4):
        copies[pair].wait()
        placed = jnp.concatenate(
            [blocks[:, 2 * pair + part].reshape(1024, 128) for part in range(2)], axis=1
        )
        straight = dot(row_table[:, :1024], placed)
        crossed = dot(row_table[:, 1024:], placed)
        for part in range(2):
            lanes = slice(part * 128, part * 128 + 128)
            value = straight[:, lanes] + pltpu.roll(crossed[:, lanes], 64, 1) * sign
            store(slice(pair * 256 + part * 128, pair * 256 + part * 128 + 128), value.astype(BF16))


def screened(middle, col_table, screen):
    facet = dot(middle, col_table)
    return times((facet[:, :512], facet[:, 512:]), (screen[0], screen[1]))


def back_other_kernel(half_ref, blocks_hbm, row_hbm, out_ref, row_table, blocks, sems, block_sems):
    (copy,) = fetch((row_hbm.at[pl.ds(half_ref[0] * 256, 256)],), (row_table,), sems)
    arriving = block_copies(blocks_hbm, blocks, block_sems)
    copy.wait()

    def store(lanes, value):
        out_ref[:, lanes] = value

    middle_rows(blocks, arriving, row_table, store)


def back_other(half, blocks, row_table):
    return pl.pallas_call(
        back_other_kernel,
        out_shape=jax.ShapeDtypeStruct((256, 1024), BF16),
        in_specs=[smem(), hbm(), hbm()],
        out_specs=vmem(),
        scratch_shapes=[
            pltpu.VMEM((256, 2048), BF16),
            pltpu.VMEM((4, 8, 4, CON, 128), BF16),
            pltpu.SemaphoreType.DMA((1,)),
            pltpu.SemaphoreType.DMA((4,)),
        ],
        compiler_params=pltpu.CompilerParams(vmem_limit_bytes=LIMIT),
        cost_estimate=pl.CostEstimate(flops=10**9, bytes_accessed=4 << 20, transcendentals=0),
        name="back_other",
    )(half, blocks, row_table)


def back_own_kernel(
    half_ref, blocks_hbm, row_hbm, col_hbm, screen_hbm, out_ref,
    row_table, blocks, col_table, screen, middle, sems, block_sems,
):
    (first,) = fetch((row_hbm.at[pl.ds(half_ref[0] * 256, 256)],), (row_table,), sems)
    arriving = block_copies(blocks_hbm, blocks, block_sems)
    copies = fetch((col_hbm, screen_hbm.at[0]), (col_table, screen), sems.at[pl.ds(1, 2)])
    first.wait()

    def store(lanes, value):
        middle[:, lanes] = value

    middle_rows(blocks, arriving, row_table, store)
    for copy in copies:
        copy.wait()
    real, imag = screened(middle[...], col_table[...], screen)
    out_ref[0] = real
    out_ref[1] = imag


def back_own(half, blocks, row_table, col_table, screen):
    return pl.pallas_call(
        back_own_kernel,
        out_shape=jax.ShapeDtypeStruct((2, 256, 512), F32),
        in_specs=[smem()] + [hbm()] * 4,
        out_specs=vmem(),
        scratch_shapes=[
            pltpu.VMEM((256, 2048), BF16),
            pltpu.VMEM((4, 8, 4, CON, 128), BF16),
            pltpu.VMEM((1024, 1024), BF16),
            pltpu.VMEM((2, 256, 512), F32),
            pltpu.VMEM((256, 1024), BF16),
            pltpu.SemaphoreType.DMA((3,)),
            pltpu.SemaphoreType.DMA((4,)),
        ],
        compiler_params=pltpu.CompilerParams(vmem_limit_bytes=LIMIT),
        cost_estimate=pl.CostEstimate(flops=2 * 10**9, bytes_accessed=8 << 20, transcendentals=0),
        name="back_own",
    )(half, blocks, row_table, col_table, screen)


def finish_kernel(middle_ref, own_ref, col_hbm, screen_hbm, out_hbm, col_table, screen, image, sems):
    copies = fetch((col_hbm, screen_hbm.at[1]), (col_table, screen), sems)
    copies[0].wait()
    copies[1].wait()
    leaving = []
    for chunk in range(2):
        rows = slice(chunk * 128, chunk * 128 + 128)
        value = screened(middle_ref[rows, :], col_table[...], (screen[0, rows, :], screen[1, rows, :]))
        for part in range(2):
            image[chunk, part] = own_ref[part, rows, :] + value[part]
        copy = pltpu.make_async_copy(image.at[chunk], out_hbm.at[:, pl.ds(chunk * 128, 128)], sems.at[2 + chunk])
        copy.start()
        leaving.append(copy)
    for copy in leaving:
        copy.wait()


def finish(middle, own, col_table, screen):
    return pl.pallas_call(
        finish_kernel,
        out_shape=jax.ShapeDtypeStruct((2, 256, 512), F32),
        in_specs=[vmem(), vmem(), hbm(), hbm()],
        out_specs=hbm(),
        scratch_shapes=[
            pltpu.VMEM((1024, 1024), BF16),
            pltpu.VMEM((2, 256, 512), F32),
            pltpu.VMEM((2, 2, 128, 512), F32),
            pltpu.SemaphoreType.DMA((4,)),
        ],
        compiler_params=pltpu.CompilerParams(vmem_limit_bytes=LIMIT),
        cost_estimate=pl.CostEstimate(flops=10**9, bytes_accessed=8 << 20, transcendentals=0),
        name="finish",
    )(middle, own, col_table, screen)


def position(x, z, y):
    return x * 32 + (z % 8) * 4 + y


GROUPS = [
    [position(x, 2 * k + l, y) for x in range(4) for l in range(2) for y in range(4)] for k in range(4)
]


def shifted(turn):
    return [
        (position(x, z, y), position(x, z + 2 * turn, y)) for x in range(4) for z in range(8) for y in range(4)
    ]


def per_device(
    visibilities, kernels, vis_offsets, block_counts,
    sub_rows, sub_cols, facet_rows, facet_cols, screen_n, layer_w,
):
    place = lax.axis_index("sf")
    group = ((place >> 3) & 3).reshape(1)
    own = pack(
        block_counts,
        visibilities.reshape(2, 8, VB), kernels.reshape(2, 8, 8, VB), vis_offsets.reshape(2, 8, VB),
    )
    packs = [lax.ppermute(own, "sf", shifted(turn)) for turn in (1, 2, 3)]
    facet_row_table, facet_col_table, begun = front_own(group, facet_rows, facet_cols, own)
    outgoing = front_others(group, packs, facet_row_table, facet_col_table, begun)
    incoming = lax.all_to_all(
        outgoing, "sf", split_axis=0, concat_axis=0, tiled=True, axis_index_groups=GROUPS
    )
    layer = lax.axis_index("wa").reshape(1)
    row_table, col_table, screen = tables(layer, sub_rows, sub_cols, layer_w, screen_n)
    blocks = incoming.reshape(4, 8, 4, CON, 128)
    theirs = back_other(1 - layer, blocks, row_table)
    received = lax.ppermute(theirs, "wa", [(0, 1), (1, 0)])
    own_part = back_own(layer, blocks, row_table, col_table, screen)
    return finish(received, own_part, col_table, screen)[:, None]


def solution(mesh):
    in_specs = (
        P(None, "sf", "wa", None, None),
        P(None, None, "sf", "wa", None, None),
        P(None, "sf", "wa", None, None),
        P("sf", "wa"),
        P(),
        P(),
        P(),
        P(),
        P("sf", None, None),
        P(),
    )
    out_specs = P(None, "sf", "wa", None)
    return jax.shard_map(
        per_device, mesh=mesh, in_specs=in_specs, out_specs=out_specs, check_vma=False
    )
```

```python
import math

import jax
import jax.numpy as jnp
from jax import lax
from jax.experimental import pallas as pl
from jax.experimental.pallas import tpu as pltpu
from jax.sharding import PartitionSpec as P

SUB = 512
CON = 64
FAC = 512
VB = 128
F32 = jnp.float32
BF16 = jnp.bfloat16
NORM = 1.0 / math.sqrt(512.0)
NN = (((1,), (0,)), ((), ()))
NT = (((1,), (1,)), ((), ()))
LIMIT = 20 << 20


def dot(first, second, numbers=NN):
    return lax.dot_general(first, second, numbers, preferred_element_type=F32)


def iota(shape, axis):
    return lax.broadcasted_iota(jnp.int32, shape, axis)


def sincos_small(theta):
    square = theta * theta
    cosine = 1.0 + square * (-0.5 + square * (1.0 / 24 + square * (-1.0 / 720 + square * (1.0 / 40320))))
    sine = theta * (1.0 + square * (-1.0 / 6 + square * (1.0 / 120 + square * (-1.0 / 5040 + square * (1.0 / 362880)))))
    return cosine, sine


def rotate_quarter(cosine, sine, quarter):
    odd = (quarter & 1) == 1
    real = jnp.where(odd, sine, cosine)
    imag = jnp.where(odd, cosine, sine)
    real = jnp.where(((quarter + 1) & 2) == 2, -real, real)
    imag = jnp.where((quarter & 2) == 2, -imag, imag)
    return real, imag


def unit_roots(steps):
    quarter = (steps + 64) >> 7
    rest = steps - (quarter << 7)
    cosine, sine = sincos_small(rest.astype(F32) * (2.0 * math.pi / 512))
    return rotate_quarter(cosine, sine, quarter)


def times(first, second):
    return (
        first[0] * second[0] - first[1] * second[1],
        first[0] * second[1] + first[1] * second[0],
    )


def cell_roots():
    low = unit_roots(iota((8, 512), 0) * iota((8, 512), 1) & 511)
    high = unit_roots(iota((8, 512), 0) * 8 * iota((8, 512), 1) & 511)
    real, imag = [], []
    for index in range(8):
        row = slice(index, index + 1)
        product = times((high[0][row], high[1][row]), low)
        real.append(product[0])
        imag.append(product[1])
    return jnp.concatenate(real, axis=0), jnp.concatenate(imag, axis=0)


def offset_roots(offsets_ref, count):
    rows = iota((count, 512), 0)
    start = jnp.zeros((count, 512), jnp.int32)
    for index in range(count):
        start = jnp.where(rows == index, offsets_ref[index], start)
    steps = start * iota((count, 512), 1)
    real, imag = unit_roots(steps & 511)
    return real * NORM, imag * NORM


def lane_steps(offsets_ref, count, width):
    shape = (8, count * width)
    lane = iota(shape, 1)
    owner = lane // width
    start = jnp.zeros(shape, jnp.int32)
    for index in range(count):
        start = jnp.where(owner == index, offsets_ref[index], start)
    return start + (lane & 63), lane


def lane_roots(frequency, lead):
    row = iota(frequency.shape, 0)
    high = unit_roots((frequency * row * 64) & 511)
    middle = unit_roots((frequency * row * 8) & 511)
    low = unit_roots((frequency * row + lead) & 511)
    low = (low[0] * NORM, low[1] * NORM)
    return high, middle, low


def row_pick(pair, index):
    return pair[0][index : index + 1], pair[1][index : index + 1]


def fetch(sources, targets, sems):
    copies = [
        pltpu.make_async_copy(source, target, sems.at[index])
        for index, (source, target) in enumerate(zip(sources, targets))
    ]
    for copy in copies:
        copy.start()
    return copies


def pack_kernel(counts, vis, kernels, all_offsets, out_ref):
    live = counts[0, 0]
    slot = iota((8, 128), 0)
    samples = [jnp.where(slot < live, vis[part].astype(F32), 0.0) for part in range(2)]
    out_ref[0:16, :] = jnp.concatenate(samples, axis=0).astype(BF16)
    for axis in range(2):
        offsets = all_offsets[axis]
        low = offsets & 7
        digits = jnp.concatenate([(offsets >> 3).astype(F32), low.astype(F32)], axis=0)
        out_ref[16 + axis * 16 : 32 + axis * 16, :] = digits.astype(BF16)
        turned = []
        for block in range(8):
            shift = (slot - low[block : block + 1, :]) & 7
            values = jnp.zeros((8, VB), F32)
            for column in range(8):
                entry = kernels[axis, column, block : block + 1, :].astype(F32)
                values = jnp.where(shift == column, entry, values)
            turned.append(values)
        out_ref[48 + axis * 64 : 112 + axis * 64, :] = jnp.concatenate(turned, axis=0).astype(BF16)


def pack(counts, vis, kernels, offsets):
    return pl.pallas_call(
        pack_kernel,
        out_shape=jax.ShapeDtypeStruct((176, 128), BF16),
        in_specs=[smem()] + [vmem()] * 3,
        out_specs=vmem(),
        compiler_params=pltpu.CompilerParams(vmem_limit_bytes=LIMIT),
        name="pack",
    )(counts, vis, kernels, offsets)


def lane_table(offsets_ref, count, width, lead, out_ref, place):
    frequency, lane = lane_steps(offsets_ref, count, width)
    high, middle, low = lane_roots(frequency, jnp.where((lane & lead) == 0, 0, 128))
    for index in range(8):
        outer = row_pick(high, index)
        for inner in range(0, 8, 2):
            first = times(times(outer, row_pick(middle, inner)), low)
            second = times(times(outer, row_pick(middle, inner + 1)), low)
            base = index * 64 + inner * 8
            for part in range(2):
                place(out_ref, part, base, jnp.concatenate([first[part], second[part]], axis=0).astype(BF16))


def grid_slot(samples, digits, kernels, row_table, col_table, spreads, turned, halves, sent):
    slot = iota((8, 128), 0)
    tile = iota((64, 8, 128), 0)
    for axis in range(2):
        for block in range(8):
            home = digits[axis][block : block + 1, :] + (digits[axis][block + 8 : block + 9, :] > slot).astype(jnp.int32)
            values = kernels[axis][block * 8 : block * 8 + 8, :]
            spreads[axis, :, block * VB : (block + 1) * VB] = (
                jnp.where(tile == home[None], values[None], 0.0).reshape(512, VB).astype(BF16)
            )
    for quarter in range(4):
        lanes = slice(quarter * 256, (quarter + 1) * 256)
        rows = dot(row_table[...], spreads[0, :, lanes])
        real_part, imag_part = (
            jnp.concatenate([samples[8 * half + 2 * quarter + part : 8 * half + 2 * quarter + part + 1] for part in range(2)], axis=1)
            for half in range(2)
        )
        real, imag = times((rows[:256], rows[256:]), (real_part, imag_part))
        turned[:256, lanes] = real.astype(BF16)
        turned[256:, lanes] = imag.astype(BF16)
    half = dot(turned[...], spreads[1], NT).astype(BF16)
    halves[:, :512] = half[:256]
    halves[:, 512:] = half[256:]
    result = dot(halves[...], col_table[...]).astype(BF16)
    for row in range(4):
        for column in range(8):
            sent[row * 8 + column] = result[row * 64 : (row + 1) * 64, column * 128 : (column + 1) * 128]


def unpacked(ref):
    return (
        ref[0:16, :].astype(F32),
        [ref[16 + axis * 16 : 32 + axis * 16, :].astype(jnp.int32) for axis in range(2)],
        [ref[48 + axis * 64 : 112 + axis * 64, :].astype(F32) for axis in range(2)],
    )


def front_scratch(slots):
    return [
        pltpu.VMEM((2, 512, 1024), BF16),
        pltpu.VMEM((512, 1024), BF16),
        pltpu.VMEM((256, 1024), BF16),
        pltpu.VMEM((slots, 32, 64, 128), BF16),
        pltpu.SemaphoreType.DMA((slots,)),
    ]


def front_own_kernel(
    group_ref, rows_ref, cols_ref, own_ref, row_out, col_out, out_hbm,
    spreads, turned, halves, sent, sems,
):
    def below(ref, part, base, value):
        ref[part * 512 + base : part * 512 + base + 16, :] = value

    lane_table(cols_ref, 8, 128, 64, col_out, below)
    base = cell_roots()
    small = offset_roots([rows_ref[4 * index + group_ref[0]] for index in range(4)], 4)
    for index in range(4):
        real, imag = times(row_pick(small, index), base)
        row_out[index * 64 : index * 64 + 64, :] = real.astype(BF16)
        row_out[256 + index * 64 : 320 + index * 64, :] = (-imag).astype(BF16)
    grid_slot(*unpacked(own_ref), row_out, col_out, spreads, turned, halves, sent.at[0])
    copy = pltpu.make_async_copy(sent.at[0], out_hbm.at[:, group_ref[0] & 3], sems.at[0])
    copy.start()
    copy.wait()


def front_own(group, facet_rows, facet_cols, own):
    return pl.pallas_call(
        front_own_kernel,
        out_shape=[
            jax.ShapeDtypeStruct((512, 512), BF16),
            jax.ShapeDtypeStruct((1024, 1024), BF16),
            jax.ShapeDtypeStruct((32, 4, 64, 128), BF16),
        ],
        in_specs=[smem(), smem(), smem(), vmem()],
        out_specs=[vmem(), vmem(), hbm()],
        scratch_shapes=front_scratch(1),
        compiler_params=pltpu.CompilerParams(vmem_limit_bytes=LIMIT),
        cost_estimate=pl.CostEstimate(flops=3 * 10**9, bytes_accessed=4 << 20, transcendentals=0),
        name="front_own",
    )(group, facet_rows, facet_cols, own)


def front_others_kernel(
    group_ref, first_ref, second_ref, third_ref, row_table, col_table, begun_hbm, out_hbm,
    spreads, turned, halves, sent, sems,
):
    copies = []
    for index, ref in enumerate((first_ref, second_ref, third_ref)):
        grid_slot(*unpacked(ref), row_table, col_table, spreads, turned, halves, sent.at[index])
        source = (group_ref[0] + 3 - index) & 3
        copy = pltpu.make_async_copy(sent.at[index], out_hbm.at[:, source], sems.at[index])
        copy.start()
        copies.append(copy)
    for copy in copies:
        copy.wait()


def front_others(group, packs, row_table, col_table, begun):
    return pl.pallas_call(
        front_others_kernel,
        out_shape=jax.ShapeDtypeStruct((32, 4, 64, 128), BF16),
        in_specs=[smem()] + [vmem()] * 5 + [hbm()],
        out_specs=hbm(),
        scratch_shapes=front_scratch(3),
        input_output_aliases={6: 0},
        compiler_params=pltpu.CompilerParams(vmem_limit_bytes=LIMIT),
        cost_estimate=pl.CostEstimate(flops=6 * 10**9, bytes_accessed=4 << 20, transcendentals=0),
        name="front_others",
    )(group, *packs, row_table, col_table, begun)


def smem():
    return pl.BlockSpec(memory_space=pltpu.SMEM)


def vmem():
    return pl.BlockSpec(memory_space=pltpu.VMEM)


def hbm():
    return pl.BlockSpec(memory_space=pltpu.HBM)


def tables_kernel(
    layer_ref, rows_ref, cols_ref, weights_ref, screen_hbm,
    high_out, base_out, small_out, cell_out, own_out, other_out, screen, sems,
):
    layer = layer_ref[0]
    (arrival,) = fetch((screen_hbm.at[0, pl.ds(layer * 256, 256)],), (screen,), sems)
    frequency, _ = lane_steps(rows_ref, 16, 64)
    high, middle, low = lane_roots(frequency, 0)
    small, cell = offset_roots(cols_ref, 8), cell_roots()
    for part in range(2):
        high_out[part] = high[part]
        small_out[part] = small[part]
        cell_out[part] = cell[part]
    for index in range(8):
        base = times(row_pick(middle, index), low)
        for part in range(2):
            base_out[part, index * 8 : index * 8 + 8, :] = base[part]
    arrival.wait()
    for side, target in enumerate((own_out, other_out)):
        weight = weights_ref[layer if side == 0 else 1 - layer] * 4.0
        for chunk in range(4):
            rows = slice(chunk * 64, (chunk + 1) * 64)
            turns = screen[rows, :] * weight
            whole = jnp.floor(turns + 0.5)
            cosine, sine = sincos_small((turns - whole) * (0.5 * math.pi))
            real, imag = rotate_quarter(cosine, sine, whole.astype(jnp.int32))
            target[0, rows, :] = real.astype(BF16)
            target[1, rows, :] = imag.astype(BF16)


def tables(layer, sub_rows, sub_cols, weights, screen):
    return pl.pallas_call(
        tables_kernel,
        out_shape=[
            jax.ShapeDtypeStruct((2, 8, 1024), F32),
            jax.ShapeDtypeStruct((2, 64, 1024), F32),
            jax.ShapeDtypeStruct((2, 8, 512), F32),
            jax.ShapeDtypeStruct((2, 64, 512), F32),
            jax.ShapeDtypeStruct((2, 256, 512), BF16),
            jax.ShapeDtypeStruct((2, 256, 512), BF16),
        ],
        in_specs=[smem(), smem(), smem(), smem(), hbm()],
        out_specs=[vmem()] * 6,
        scratch_shapes=[pltpu.VMEM((256, 512), F32), pltpu.SemaphoreType.DMA((1,))],
        compiler_params=pltpu.CompilerParams(vmem_limit_bytes=LIMIT),
        cost_estimate=pl.CostEstimate(flops=10**9, bytes_accessed=8 << 20, transcendentals=0),
        name="tables",
    )(layer, sub_rows, sub_cols, weights, screen)


def middle_rows(half, blocks, high, base, row_table, store):
    for index in range(4):
        row = pl.ds(half * 4 + index, 1)
        value = times((high[0, row, :], high[1, row, :]), (base[0], base[1]))
        for part in range(2):
            row_table[index * 64 : index * 64 + 64, part * 1024 : part * 1024 + 1024] = value[part].astype(BF16)
    sign = jnp.where((iota((1, 128), 1) & 64) == 0, -1.0, 1.0)
    for pair in range(4):
        placed = jnp.concatenate(
            [blocks[:, 2 * pair + part].reshape(1024, 128) for part in range(2)], axis=1
        )
        straight = dot(row_table[:, :1024], placed)
        crossed = dot(row_table[:, 1024:], placed)
        for part in range(2):
            lanes = slice(part * 128, part * 128 + 128)
            value = straight[:, lanes] + pltpu.roll(crossed[:, lanes], 64, 1) * sign
            store(slice(pair * 256 + part * 128, pair * 256 + part * 128 + 128), value.astype(BF16))


def screened(middle, col_table, screen):
    facet = dot(middle, col_table)
    return times((facet[:, :512], facet[:, 512:]), (screen[0].astype(F32), screen[1].astype(F32)))


def back_other_kernel(half_ref, blocks, high, base, out_ref, row_table):
    def store(lanes, value):
        out_ref[:, lanes] = value

    middle_rows(half_ref[0], blocks, high, base, row_table, store)


def back_other(half, blocks, high, base):
    return pl.pallas_call(
        back_other_kernel,
        out_shape=jax.ShapeDtypeStruct((256, 1024), BF16),
        in_specs=[smem()] + [vmem()] * 3,
        out_specs=vmem(),
        scratch_shapes=[pltpu.VMEM((256, 2048), BF16)],
        compiler_params=pltpu.CompilerParams(vmem_limit_bytes=LIMIT),
        cost_estimate=pl.CostEstimate(flops=10**9, bytes_accessed=4 << 20, transcendentals=0),
        name="back_other",
    )(half, blocks, high, base)


def back_own_kernel(half_ref, blocks, high, base, small, cell, screen, out_ref, col_out, row_table, middle):
    def store(lanes, value):
        middle[:, lanes] = value

    middle_rows(half_ref[0], blocks, high, base, row_table, store)
    for column in range(8):
        row = slice(column, column + 1)
        value = times((small[0, row, :], small[1, row, :]), (cell[0], cell[1]))
        real, imag = value[0].astype(BF16), value[1].astype(BF16)
        rows = slice(column * 128, column * 128 + 64)
        col_out[rows, :512] = real
        col_out[rows, 512:] = imag
        rows = slice(column * 128 + 64, column * 128 + 128)
        col_out[rows, :512] = -imag
        col_out[rows, 512:] = real
    real, imag = screened(middle[...], col_out[...], screen)
    out_ref[0] = real
    out_ref[1] = imag


def back_own(half, blocks, high, base, small, cell, screen):
    return pl.pallas_call(
        back_own_kernel,
        out_shape=[
            jax.ShapeDtypeStruct((2, 256, 512), F32),
            jax.ShapeDtypeStruct((1024, 1024), BF16),
        ],
        in_specs=[smem()] + [vmem()] * 6,
        out_specs=[vmem(), vmem()],
        scratch_shapes=[pltpu.VMEM((256, 2048), BF16), pltpu.VMEM((256, 1024), BF16)],
        compiler_params=pltpu.CompilerParams(vmem_limit_bytes=LIMIT),
        cost_estimate=pl.CostEstimate(flops=2 * 10**9, bytes_accessed=8 << 20, transcendentals=0),
        name="back_own",
    )(half, blocks, high, base, small, cell, screen)


def finish_kernel(middle_ref, own_ref, col_ref, screen_ref, out_hbm, image, sems):
    leaving = []
    for chunk in range(2):
        rows = slice(chunk * 128, chunk * 128 + 128)
        value = screened(middle_ref[rows, :], col_ref[...], (screen_ref[0, rows, :], screen_ref[1, rows, :]))
        for part in range(2):
            image[chunk, part] = own_ref[part, rows, :] + value[part]
        copy = pltpu.make_async_copy(image.at[chunk], out_hbm.at[:, pl.ds(chunk * 128, 128)], sems.at[chunk])
        copy.start()
        leaving.append(copy)
    for copy in leaving:
        copy.wait()


def finish(middle, own, col_table, screen):
    return pl.pallas_call(
        finish_kernel,
        out_shape=jax.ShapeDtypeStruct((2, 256, 512), F32),
        in_specs=[vmem()] * 4,
        out_specs=hbm(),
        scratch_shapes=[pltpu.VMEM((2, 2, 128, 512), F32), pltpu.SemaphoreType.DMA((2,))],
        compiler_params=pltpu.CompilerParams(vmem_limit_bytes=LIMIT),
        cost_estimate=pl.CostEstimate(flops=10**9, bytes_accessed=8 << 20, transcendentals=0),
        name="finish",
    )(middle, own, col_table, screen)


def position(x, z, y):
    return x * 32 + (z % 8) * 4 + y


GROUPS = [
    [position(x, 2 * k + l, y) for x in range(4) for l in range(2) for y in range(4)] for k in range(4)
]


def shifted(turn):
    return [
        (position(x, z, y), position(x, z + 2 * turn, y)) for x in range(4) for z in range(8) for y in range(4)
    ]


def per_device(
    visibilities, kernels, vis_offsets, block_counts,
    sub_rows, sub_cols, facet_rows, facet_cols, screen_n, layer_w,
):
    place = lax.axis_index("sf")
    group = ((place >> 3) & 3).reshape(1)
    own = pack(
        block_counts,
        visibilities.reshape(2, 8, VB), kernels.reshape(2, 8, 8, VB), vis_offsets.reshape(2, 8, VB),
    )
    packs = [lax.ppermute(own, "sf", shifted(turn)) for turn in (1, 2, 3)]
    facet_row_table, facet_col_table, begun = front_own(group, facet_rows, facet_cols, own)
    outgoing = front_others(group, packs, facet_row_table, facet_col_table, begun)
    incoming = lax.all_to_all(
        outgoing, "sf", split_axis=0, concat_axis=0, tiled=True, axis_index_groups=GROUPS
    )
    layer = lax.axis_index("wa").reshape(1)
    high, base, small, cell, own_screen, other_screen = tables(layer, sub_rows, sub_cols, layer_w, screen_n)
    blocks = incoming.reshape(4, 8, 4, CON, 128)
    theirs = back_other(1 - layer, blocks, high, base)
    received = lax.ppermute(theirs, "wa", [(0, 1), (1, 0)])
    own_part, col_table = back_own(layer, blocks, high, base, small, cell, own_screen)
    return finish(received, own_part, col_table, other_screen)[:, None]


def solution(mesh):
    in_specs = (
        P(None, "sf", "wa", None, None),
        P(None, None, "sf", "wa", None, None),
        P(None, "sf", "wa", None, None),
        P("sf", "wa"),
        P(),
        P(),
        P(),
        P(),
        P("sf", None, None),
        P(),
    )
    out_specs = P(None, "sf", "wa", None)
    return jax.shard_map(
        per_device, mesh=mesh, in_specs=in_specs, out_specs=out_specs, check_vma=False
    )
```

```python
import math

import jax
import jax.numpy as jnp
from jax import lax
from jax.experimental import pallas as pl
from jax.experimental.pallas import tpu as pltpu
from jax.sharding import PartitionSpec as P

SUB = 512
CON = 64
FAC = 512
VB = 128
F32 = jnp.float32
BF16 = jnp.bfloat16
NORM = 1.0 / math.sqrt(512.0)
NN = (((1,), (0,)), ((), ()))
NT = (((1,), (1,)), ((), ()))
LIMIT = 20 << 20


def dot(first, second, numbers=NN):
    return lax.dot_general(first, second, numbers, preferred_element_type=F32)


def iota(shape, axis):
    return lax.broadcasted_iota(jnp.int32, shape, axis)


def sincos_small(theta):
    square = theta * theta
    cosine = 1.0 + square * (-0.5 + square * (1.0 / 24 + square * (-1.0 / 720 + square * (1.0 / 40320))))
    sine = theta * (1.0 + square * (-1.0 / 6 + square * (1.0 / 120 + square * (-1.0 / 5040 + square * (1.0 / 362880)))))
    return cosine, sine


def rotate_quarter(cosine, sine, quarter):
    odd = (quarter & 1) == 1
    real = jnp.where(odd, sine, cosine)
    imag = jnp.where(odd, cosine, sine)
    real = jnp.where(((quarter + 1) & 2) == 2, -real, real)
    imag = jnp.where((quarter & 2) == 2, -imag, imag)
    return real, imag


def unit_roots(steps):
    quarter = (steps + 64) >> 7
    rest = steps - (quarter << 7)
    cosine, sine = sincos_small(rest.astype(F32) * (2.0 * math.pi / 512))
    return rotate_quarter(cosine, sine, quarter)


def times(first, second):
    return (
        first[0] * second[0] - first[1] * second[1],
        first[0] * second[1] + first[1] * second[0],
    )


def picked(ref, first, count):
    return [ref[first + index] for index in range(count)]


def cell_roots():
    low = unit_roots(iota((8, 512), 0) * iota((8, 512), 1) & 511)
    high = unit_roots(iota((8, 512), 0) * 8 * iota((8, 512), 1) & 511)
    real, imag = [], []
    for index in range(8):
        row = slice(index, index + 1)
        product = times((high[0][row], high[1][row]), low)
        real.append(product[0])
        imag.append(product[1])
    return jnp.concatenate(real, axis=0), jnp.concatenate(imag, axis=0)


def offset_roots(offsets_ref, count):
    rows = iota((count, 512), 0)
    start = jnp.zeros((count, 512), jnp.int32)
    for index in range(count):
        start = jnp.where(rows == index, offsets_ref[index], start)
    steps = start * iota((count, 512), 1)
    real, imag = unit_roots(steps & 511)
    return real * NORM, imag * NORM


def lane_steps(offsets_ref, count, width):
    shape = (8, count * width)
    lane = iota(shape, 1)
    owner = lane // width
    start = jnp.zeros(shape, jnp.int32)
    for index in range(count):
        start = jnp.where(owner == index, offsets_ref[index], start)
    return start + (lane & 63), lane


def lane_roots(frequency, lead):
    row = iota(frequency.shape, 0)
    high = unit_roots((frequency * row * 64) & 511)
    middle = unit_roots((frequency * row * 8) & 511)
    low = unit_roots((frequency * row + lead) & 511)
    low = (low[0] * NORM, low[1] * NORM)
    return high, middle, low


def row_pick(pair, index):
    return pair[0][index : index + 1], pair[1][index : index + 1]


def fetch(sources, targets, sems):
    copies = [
        pltpu.make_async_copy(source, target, sems.at[index])
        for index, (source, target) in enumerate(zip(sources, targets))
    ]
    for copy in copies:
        copy.start()
    return copies


def pack_kernel(counts, vis, kernels, all_offsets, out_ref):
    live = counts[0, 0]
    slot = iota((8, 128), 0)
    samples = [jnp.where(slot < live, vis[part].astype(F32), 0.0) for part in range(2)]
    out_ref[0:16, :] = jnp.concatenate(samples, axis=0).astype(BF16)
    for axis in range(2):
        offsets = all_offsets[axis]
        low = offsets & 7
        digits = jnp.concatenate([(offsets >> 3).astype(F32), low.astype(F32)], axis=0)
        out_ref[16 + axis * 16 : 32 + axis * 16, :] = digits.astype(BF16)
        turned = []
        for block in range(8):
            shift = (slot - low[block : block + 1, :]) & 7
            values = jnp.zeros((8, VB), F32)
            for column in range(8):
                entry = kernels[axis, column, block : block + 1, :].astype(F32)
                values = jnp.where(shift == column, entry, values)
            turned.append(values)
        out_ref[48 + axis * 64 : 112 + axis * 64, :] = jnp.concatenate(turned, axis=0).astype(BF16)


def pack(counts, vis, kernels, offsets):
    return pl.pallas_call(
        pack_kernel,
        out_shape=jax.ShapeDtypeStruct((176, 128), BF16),
        in_specs=[smem()] + [vmem()] * 3,
        out_specs=vmem(),
        compiler_params=pltpu.CompilerParams(vmem_limit_bytes=LIMIT),
        name="pack",
    )(counts, vis, kernels, offsets)


def lane_table(offsets_ref, count, width, lead, out_ref, place):
    frequency, lane = lane_steps(offsets_ref, count, width)
    high, middle, low = lane_roots(frequency, jnp.where((lane & lead) == 0, 0, 128))
    for index in range(8):
        outer = row_pick(high, index)
        for inner in range(0, 8, 2):
            first = times(times(outer, row_pick(middle, inner)), low)
            second = times(times(outer, row_pick(middle, inner + 1)), low)
            base = index * 64 + inner * 8
            for part in range(2):
                place(out_ref, part, base, jnp.concatenate([first[part], second[part]], axis=0).astype(BF16))


def spread_block(data, axis, block, spread):
    _, digits, kernels = data
    tile = iota((64, 8, 128), 0)
    home = digits[axis][block : block + 1, :] + (
        digits[axis][block + 8 : block + 9, :] > iota((8, 128), 0)
    ).astype(jnp.int32)
    values = kernels[axis][block * 8 : block * 8 + 8, :]
    spread[axis, :, block * VB : (block + 1) * VB] = (
        jnp.where(tile == home[None], values[None], 0.0).reshape(512, VB).astype(BF16)
    )


def turn_rows(data, quarter, row_table, spread, turned):
    samples = data[0]
    lanes = slice(quarter * 256, (quarter + 1) * 256)
    rows = dot(row_table[...], spread[0, :, lanes])
    real_part, imag_part = (
        jnp.concatenate([samples[8 * half + 2 * quarter + part : 8 * half + 2 * quarter + part + 1] for part in range(2)], axis=1)
        for half in range(2)
    )
    real, imag = times((rows[:256], rows[256:]), (real_part, imag_part))
    turned[:256, lanes] = real.astype(BF16)
    turned[256:, lanes] = imag.astype(BF16)


def peer(row, column):
    return (column & 3) * 8 + (column >> 2) * 4 + row


def grid_slots(refs, row_table, col_table, spread, turned, halves, store):
    for index, ref in enumerate(refs):
        data = unpacked(ref)
        for axis in range(2):
            for block in range(8):
                spread_block(data, axis, block, spread)
        for quarter in range(4):
            turn_rows(data, quarter, row_table, spread, turned)
        half = dot(turned[...], spread[1], NT).astype(BF16)
        halves[index * 256 : index * 256 + 256, :512] = half[:256]
        halves[index * 256 : index * 256 + 256, 512:] = half[256:]
    for pair in range(4):
        result = dot(halves[...], col_table[:, pair * 256 : pair * 256 + 256]).astype(BF16)
        for index in range(len(refs)):
            for row in range(4):
                for part in range(2):
                    start = index * 256 + row * 64
                    value = result[start : start + 64, part * 128 : (part + 1) * 128]
                    store(index, peer(row, 2 * pair + part), value)


def unpacked(ref):
    return (
        ref[0:16, :].astype(F32),
        [ref[16 + axis * 16 : 32 + axis * 16, :].astype(jnp.int32) for axis in range(2)],
        [ref[48 + axis * 64 : 112 + axis * 64, :].astype(F32) for axis in range(2)],
    )


def front_scratch(slots):
    return [
        pltpu.VMEM((2, 512, 1024), BF16),
        pltpu.VMEM((512, 1024), BF16),
        pltpu.VMEM((slots * 256, 1024), BF16),
    ]


def front_own_kernel(
    group_ref, offsets_ref, own_ref, row_out, col_out, out_ref, spreads, turned, halves,
):
    def below(ref, part, base, value):
        ref[part * 512 + base : part * 512 + base + 16, :] = value

    lane_table(picked(offsets_ref, 16, 8), 8, 128, 64, col_out, below)
    base = cell_roots()
    small = offset_roots([offsets_ref[4 * index + group_ref[0]] for index in range(4)], 4)
    for index in range(4):
        real, imag = times(row_pick(small, index), base)
        row_out[index * 64 : index * 64 + 64, :] = real.astype(BF16)
        row_out[256 + index * 64 : 320 + index * 64, :] = (-imag).astype(BF16)

    def store(index, facet, value):
        out_ref[facet] = value

    grid_slots([own_ref], row_out, col_out, spreads, turned, halves, store)


def front_own(group, offsets, own):
    return pl.pallas_call(
        front_own_kernel,
        out_shape=[
            jax.ShapeDtypeStruct((512, 512), BF16),
            jax.ShapeDtypeStruct((1024, 1024), BF16),
            jax.ShapeDtypeStruct((32, 64, 128), BF16),
        ],
        in_specs=[smem(), smem(), vmem()],
        out_specs=[vmem()] * 3,
        scratch_shapes=front_scratch(1),
        compiler_params=pltpu.CompilerParams(vmem_limit_bytes=LIMIT),
        cost_estimate=pl.CostEstimate(flops=3 * 10**9, bytes_accessed=4 << 20, transcendentals=0),
        name="front_own",
    )(group, offsets, own)


def front_others_kernel(
    group_ref, first_ref, second_ref, third_ref, row_table, col_table, own_ref, out_ref, spreads, turned, halves,
):
    group = group_ref[0]
    for facet in range(32):
        out_ref[facet, group & 3] = own_ref[facet]

    def store(index, facet, value):
        out_ref[facet, (group + 3 - index) & 3] = value

    grid_slots([first_ref, second_ref, third_ref], row_table, col_table, spreads, turned, halves, store)


def front_others(group, packs, row_table, col_table, own):
    return pl.pallas_call(
        front_others_kernel,
        out_shape=jax.ShapeDtypeStruct((32, 4, 64, 128), BF16),
        in_specs=[smem()] + [vmem()] * 6,
        out_specs=vmem(),
        scratch_shapes=front_scratch(3),
        compiler_params=pltpu.CompilerParams(vmem_limit_bytes=LIMIT),
        cost_estimate=pl.CostEstimate(flops=6 * 10**9, bytes_accessed=4 << 20, transcendentals=0),
        name="front_others",
    )(group, *packs, row_table, col_table, own)


def smem():
    return pl.BlockSpec(memory_space=pltpu.SMEM)


def vmem():
    return pl.BlockSpec(memory_space=pltpu.VMEM)


def hbm():
    return pl.BlockSpec(memory_space=pltpu.HBM)


def tables_kernel(
    layer_ref, offsets_ref, weights_ref, screen_hbm,
    high_out, base_out, small_out, cell_out, own_out, other_out, screen, sems,
):
    layer = layer_ref[0]
    (arrival,) = fetch((screen_hbm.at[0, pl.ds(layer * 256, 256)],), (screen,), sems)
    frequency, _ = lane_steps(picked(offsets_ref, 24, 16), 16, 64)
    high, middle, low = lane_roots(frequency, 0)
    small, cell = offset_roots(picked(offsets_ref, 40, 8), 8), cell_roots()
    for part in range(2):
        high_out[part] = high[part]
        small_out[part] = small[part]
        cell_out[part] = cell[part]
    for index in range(8):
        base = times(row_pick(middle, index), low)
        for part in range(2):
            base_out[part, index * 8 : index * 8 + 8, :] = base[part]
    arrival.wait()
    for side, target in enumerate((own_out, other_out)):
        weight = weights_ref[layer if side == 0 else 1 - layer] * 4.0
        for chunk in range(4):
            rows = slice(chunk * 64, (chunk + 1) * 64)
            turns = screen[rows, :] * weight
            whole = jnp.floor(turns + 0.5)
            cosine, sine = sincos_small((turns - whole) * (0.5 * math.pi))
            real, imag = rotate_quarter(cosine, sine, whole.astype(jnp.int32))
            target[0, rows, :] = real.astype(BF16)
            target[1, rows, :] = imag.astype(BF16)


def tables(layer, offsets, weights, screen):
    return pl.pallas_call(
        tables_kernel,
        out_shape=[
            jax.ShapeDtypeStruct((2, 8, 1024), F32),
            jax.ShapeDtypeStruct((2, 64, 1024), F32),
            jax.ShapeDtypeStruct((2, 8, 512), F32),
            jax.ShapeDtypeStruct((2, 64, 512), F32),
            jax.ShapeDtypeStruct((2, 256, 512), BF16),
            jax.ShapeDtypeStruct((2, 256, 512), BF16),
        ],
        in_specs=[smem(), smem(), smem(), hbm()],
        out_specs=[vmem()] * 6,
        scratch_shapes=[pltpu.VMEM((256, 512), F32), pltpu.SemaphoreType.DMA((1,))],
        compiler_params=pltpu.CompilerParams(vmem_limit_bytes=LIMIT),
        cost_estimate=pl.CostEstimate(flops=10**9, bytes_accessed=8 << 20, transcendentals=0),
        name="tables",
    )(layer, offsets, weights, screen)


def middle_rows(half, blocks, high, base, row_table, store):
    for index in range(4):
        row = pl.ds(half * 4 + index, 1)
        value = times((high[0, row, :], high[1, row, :]), (base[0], base[1]))
        for part in range(2):
            row_table[part * 256 + index * 64 : part * 256 + index * 64 + 64, :] = value[part].astype(BF16)
    sign = jnp.where((iota((1, 128), 1) & 64) == 0, -1.0, 1.0)
    for pair in range(4):
        placed = jnp.concatenate(
            [blocks[(2 * pair + part) & 3, pair >> 1].reshape(1024, 128) for part in range(2)], axis=1
        )
        both = dot(row_table[...], placed)
        straight, crossed = both[:256], both[256:]
        for part in range(2):
            lanes = slice(part * 128, part * 128 + 128)
            value = straight[:, lanes] + pltpu.roll(crossed[:, lanes], 64, 1) * sign
            store(slice(pair * 256 + part * 128, pair * 256 + part * 128 + 128), value.astype(BF16))


def screened(middle, col_table, screen):
    facet = dot(middle, col_table)
    return times((facet[:, :512], facet[:, 512:]), (screen[0].astype(F32), screen[1].astype(F32)))


def back_other_kernel(half_ref, blocks, high, base, out_ref, row_table):
    def store(lanes, value):
        out_ref[:, lanes] = value

    middle_rows(half_ref[0], blocks, high, base, row_table, store)


def back_other(half, blocks, high, base):
    return pl.pallas_call(
        back_other_kernel,
        out_shape=jax.ShapeDtypeStruct((256, 1024), BF16),
        in_specs=[smem()] + [vmem()] * 3,
        out_specs=vmem(),
        scratch_shapes=[pltpu.VMEM((512, 1024), BF16)],
        compiler_params=pltpu.CompilerParams(vmem_limit_bytes=LIMIT),
        cost_estimate=pl.CostEstimate(flops=10**9, bytes_accessed=4 << 20, transcendentals=0),
        name="back_other",
    )(half, blocks, high, base)


def back_own_kernel(half_ref, blocks, high, base, small, cell, screen, out_ref, col_out, row_table, middle):
    def store(lanes, value):
        middle[:, lanes] = value

    middle_rows(half_ref[0], blocks, high, base, row_table, store)
    for column in range(8):
        row = slice(column, column + 1)
        value = times((small[0, row, :], small[1, row, :]), (cell[0], cell[1]))
        real, imag = value[0].astype(BF16), value[1].astype(BF16)
        rows = slice(column * 128, column * 128 + 64)
        col_out[rows, :512] = real
        col_out[rows, 512:] = imag
        rows = slice(column * 128 + 64, column * 128 + 128)
        col_out[rows, :512] = -imag
        col_out[rows, 512:] = real
    real, imag = screened(middle[...], col_out[...], screen)
    out_ref[0] = real
    out_ref[1] = imag


def back_own(half, blocks, high, base, small, cell, screen):
    return pl.pallas_call(
        back_own_kernel,
        out_shape=[
            jax.ShapeDtypeStruct((2, 256, 512), F32),
            jax.ShapeDtypeStruct((1024, 1024), BF16),
        ],
        in_specs=[smem()] + [vmem()] * 6,
        out_specs=[vmem(), vmem()],
        scratch_shapes=[pltpu.VMEM((512, 1024), BF16), pltpu.VMEM((256, 1024), BF16)],
        compiler_params=pltpu.CompilerParams(vmem_limit_bytes=LIMIT),
        cost_estimate=pl.CostEstimate(flops=2 * 10**9, bytes_accessed=8 << 20, transcendentals=0),
        name="back_own",
    )(half, blocks, high, base, small, cell, screen)


def finish_kernel(middle_ref, own_ref, col_ref, screen_ref, out_hbm, image, sems):
    leaving = []
    for chunk in range(2):
        lanes = slice(chunk * 256, chunk * 256 + 256)
        facet = [dot(middle_ref[...], col_ref[:, part * 512 + chunk * 256 : part * 512 + chunk * 256 + 256]) for part in range(2)]
        value = times(facet, [screen_ref[part, :, lanes].astype(F32) for part in range(2)])
        for part in range(2):
            image[chunk, part] = own_ref[part, :, lanes] + value[part]
        copy = pltpu.make_async_copy(image.at[chunk], out_hbm.at[:, :, pl.ds(chunk * 256, 256)], sems.at[chunk])
        copy.start()
        leaving.append(copy)
    for copy in leaving:
        copy.wait()


def finish(middle, own, col_table, screen):
    return pl.pallas_call(
        finish_kernel,
        out_shape=jax.ShapeDtypeStruct((2, 256, 512), F32),
        in_specs=[vmem()] * 4,
        out_specs=hbm(),
        scratch_shapes=[pltpu.VMEM((2, 2, 256, 256), F32), pltpu.SemaphoreType.DMA((2,))],
        compiler_params=pltpu.CompilerParams(vmem_limit_bytes=LIMIT),
        cost_estimate=pl.CostEstimate(flops=10**9, bytes_accessed=8 << 20, transcendentals=0),
        name="finish",
    )(middle, own, col_table, screen)


def position(x, z, y):
    return x * 32 + (z % 8) * 4 + y


GROUPS = [
    [position(x, 2 * k + l, y) for y in range(4) for l in range(2) for x in range(4)] for k in range(4)
]


def shifted(turn):
    return [
        (position(x, z, y), position(x, z + 2 * turn, y)) for x in range(4) for z in range(8) for y in range(4)
    ]


def per_device(
    visibilities, kernels, vis_offsets, block_counts,
    sub_rows, sub_cols, facet_rows, facet_cols, screen_n, layer_w,
):
    place = lax.axis_index("sf")
    group = ((place >> 3) & 3).reshape(1)
    own = pack(
        block_counts,
        visibilities.reshape(2, 8, VB), kernels.reshape(2, 8, 8, VB), vis_offsets.reshape(2, 8, VB),
    )
    offsets = jnp.concatenate([facet_rows, facet_cols, sub_rows, sub_cols])
    packs = [lax.ppermute(own, "sf", shifted(turn)) for turn in (1, 2, 3)]
    facet_row_table, facet_col_table, own_sent = front_own(group, offsets, own)
    outgoing = front_others(group, packs, facet_row_table, facet_col_table, own_sent)
    incoming = lax.all_to_all(
        outgoing, "sf", split_axis=0, concat_axis=0, tiled=True, axis_index_groups=GROUPS
    )
    layer = lax.axis_index("wa").reshape(1)
    high, base, small, cell, own_screen, other_screen = tables(layer, offsets, layer_w, screen_n)
    blocks = incoming.reshape(4, 2, 4, 4, CON, 128)
    theirs = back_other(1 - layer, blocks, high, base)
    received = lax.ppermute(theirs, "wa", [(0, 1), (1, 0)])
    own_part, col_table = back_own(layer, blocks, high, base, small, cell, own_screen)
    return finish(received, own_part, col_table, other_screen)[:, None]


def solution(mesh):
    in_specs = (
        P(None, "sf", "wa", None, None),
        P(None, None, "sf", "wa", None, None),
        P(None, "sf", "wa", None, None),
        P("sf", "wa"),
        P(),
        P(),
        P(),
        P(),
        P("sf", None, None),
        P(),
    )
    out_specs = P(None, "sf", "wa", None)
    return jax.shard_map(
        per_device, mesh=mesh, in_specs=in_specs, out_specs=out_specs, check_vma=False
    )
```

```python
import math

import jax
import jax.numpy as jnp
from jax import lax
from jax.experimental import pallas as pl
from jax.experimental.pallas import tpu as pltpu
from jax.sharding import PartitionSpec as P

SUB = 512
CON = 64
FAC = 512
VB = 128
F32 = jnp.float32
BF16 = jnp.bfloat16
NORM = 1.0 / math.sqrt(512.0)
NN = (((1,), (0,)), ((), ()))
NT = (((1,), (1,)), ((), ()))
LIMIT = 20 << 20


def dot(first, second, numbers=NN):
    return lax.dot_general(first, second, numbers, preferred_element_type=F32)


def iota(shape, axis):
    return lax.broadcasted_iota(jnp.int32, shape, axis)


def sincos_small(theta):
    square = theta * theta
    cosine = 1.0 + square * (-0.5 + square * (1.0 / 24 + square * (-1.0 / 720 + square * (1.0 / 40320))))
    sine = theta * (1.0 + square * (-1.0 / 6 + square * (1.0 / 120 + square * (-1.0 / 5040 + square * (1.0 / 362880)))))
    return cosine, sine


def rotate_quarter(cosine, sine, quarter):
    odd = (quarter & 1) == 1
    real = jnp.where(odd, sine, cosine)
    imag = jnp.where(odd, cosine, sine)
    real = jnp.where(((quarter + 1) & 2) == 2, -real, real)
    imag = jnp.where((quarter & 2) == 2, -imag, imag)
    return real, imag


def unit_roots(steps):
    quarter = (steps + 64) >> 7
    rest = steps - (quarter << 7)
    cosine, sine = sincos_small(rest.astype(F32) * (2.0 * math.pi / 512))
    return rotate_quarter(cosine, sine, quarter)


def times(first, second):
    return (
        first[0] * second[0] - first[1] * second[1],
        first[0] * second[1] + first[1] * second[0],
    )


def picked(ref, first, count):
    return [ref[first + index] for index in range(count)]


def cell_roots():
    low = unit_roots(iota((8, 512), 0) * iota((8, 512), 1) & 511)
    high = unit_roots(iota((8, 512), 0) * 8 * iota((8, 512), 1) & 511)
    real, imag = [], []
    for index in range(8):
        row = slice(index, index + 1)
        product = times((high[0][row], high[1][row]), low)
        real.append(product[0])
        imag.append(product[1])
    return jnp.concatenate(real, axis=0), jnp.concatenate(imag, axis=0)


def offset_roots(offsets_ref, count):
    rows = iota((count, 512), 0)
    start = jnp.zeros((count, 512), jnp.int32)
    for index in range(count):
        start = jnp.where(rows == index, offsets_ref[index], start)
    steps = start * iota((count, 512), 1)
    real, imag = unit_roots(steps & 511)
    return real * NORM, imag * NORM


def lane_steps(offsets_ref, count, width):
    shape = (8, count * width)
    lane = iota(shape, 1)
    owner = lane // width
    start = jnp.zeros(shape, jnp.int32)
    for index in range(count):
        start = jnp.where(owner == index, offsets_ref[index], start)
    return start + (lane & 63), lane


def lane_roots(frequency, lead):
    row = iota(frequency.shape, 0)
    high = unit_roots((frequency * row * 64) & 511)
    middle = unit_roots((frequency * row * 8) & 511)
    low = unit_roots((frequency * row + lead) & 511)
    low = (low[0] * NORM, low[1] * NORM)
    return high, middle, low


def row_pick(pair, index):
    return pair[0][index : index + 1], pair[1][index : index + 1]


def fetch(sources, targets, sems):
    copies = [
        pltpu.make_async_copy(source, target, sems.at[index])
        for index, (source, target) in enumerate(zip(sources, targets))
    ]
    for copy in copies:
        copy.start()
    return copies


def pack_kernel(counts, inputs, out_ref):
    live = counts[0, 0]
    slot = iota((8, 128), 0)
    vis = inputs[0:16, :].astype(F32)
    kernels = inputs[16:144, :].astype(F32)
    high = inputs[144:160, :].astype(F32)
    low = inputs[160:176, :].astype(F32)
    samples = [jnp.where(slot < live, vis[part * 8 : part * 8 + 8], 0.0) for part in range(2)]
    out_ref[0:16, :] = jnp.concatenate(samples, axis=0).astype(BF16)
    for axis in range(2):
        rows = slice(axis * 8, axis * 8 + 8)
        digits = jnp.concatenate([high[rows], low[rows]], axis=0)
        out_ref[16 + axis * 16 : 32 + axis * 16, :] = digits.astype(BF16)
        turned = []
        for block in range(8):
            shift = (slot - low[axis * 8 + block : axis * 8 + block + 1, :].astype(jnp.int32)) & 7
            values = jnp.zeros((8, VB), F32)
            for column in range(8):
                row = axis * 64 + column * 8 + block
                values = jnp.where(shift == column, kernels[row : row + 1, :], values)
            turned.append(values)
        out_ref[48 + axis * 64 : 112 + axis * 64, :] = jnp.concatenate(turned, axis=0).astype(BF16)


def pack(counts, vis, kernels, offsets):
    inputs = jnp.concatenate(
        [
            vis.reshape(16, VB), kernels.reshape(128, VB),
            (offsets >> 3).astype(BF16).reshape(16, VB), (offsets & 7).astype(BF16).reshape(16, VB),
        ]
    )
    return pl.pallas_call(
        pack_kernel,
        out_shape=jax.ShapeDtypeStruct((176, 128), BF16),
        in_specs=[smem(), vmem()],
        out_specs=vmem(),
        compiler_params=pltpu.CompilerParams(vmem_limit_bytes=LIMIT),
        name="pack",
    )(counts, inputs)


def lane_table(offsets_ref, count, width, lead, out_ref, place):
    frequency, lane = lane_steps(offsets_ref, count, width)
    high, middle, low = lane_roots(frequency, jnp.where((lane & lead) == 0, 0, 128))
    for index in range(8):
        outer = row_pick(high, index)
        for inner in range(0, 8, 2):
            first = times(times(outer, row_pick(middle, inner)), low)
            second = times(times(outer, row_pick(middle, inner + 1)), low)
            base = index * 64 + inner * 8
            for part in range(2):
                place(out_ref, part, base, jnp.concatenate([first[part], second[part]], axis=0).astype(BF16))


def spread_block(data, axis, block, spread):
    _, digits, kernels = data
    tile = iota((64, 8, 128), 0)
    home = digits[axis][block : block + 1, :] + (
        digits[axis][block + 8 : block + 9, :] > iota((8, 128), 0)
    ).astype(jnp.int32)
    values = kernels[axis][block * 8 : block * 8 + 8, :]
    spread[axis, :, block * VB : (block + 1) * VB] = (
        jnp.where(tile == home[None], values[None], 0.0).reshape(512, VB).astype(BF16)
    )


def turn_rows(data, quarter, row_table, spread, turned):
    samples = data[0]
    lanes = slice(quarter * 256, (quarter + 1) * 256)
    rows = dot(row_table[...], spread[0, :, lanes])
    real_part, imag_part = (
        jnp.concatenate([samples[8 * half + 2 * quarter + part : 8 * half + 2 * quarter + part + 1] for part in range(2)], axis=1)
        for half in range(2)
    )
    real, imag = times((rows[:256], rows[256:]), (real_part, imag_part))
    turned[:256, lanes] = real.astype(BF16)
    turned[256:, lanes] = imag.astype(BF16)


def peer(row, column):
    return (column >> 2) * 16 + (column & 3) * 4 + row * 1


def grid_slots(refs, row_table, col_table, spread, turned, halves, store):
    for index, ref in enumerate(refs):
        data = unpacked(ref)
        for axis in range(2):
            for block in range(8):
                spread_block(data, axis, block, spread)
        for quarter in range(4):
            turn_rows(data, quarter, row_table, spread, turned)
        half = dot(turned[...], spread[1], NT).astype(BF16)
        halves[index * 256 : index * 256 + 256, :512] = half[:256]
        halves[index * 256 : index * 256 + 256, 512:] = half[256:]
    for pair in range(4):
        result = dot(halves[...], col_table[:, pair * 256 : pair * 256 + 256]).astype(BF16)
        for index in range(len(refs)):
            for row in range(4):
                for part in range(2):
                    start = index * 256 + row * 64
                    value = result[start : start + 64, part * 128 : (part + 1) * 128]
                    store(index, peer(row, 2 * pair + part), value)


def unpacked(ref):
    return (
        ref[0:16, :].astype(F32),
        [ref[16 + axis * 16 : 32 + axis * 16, :].astype(jnp.int32) for axis in range(2)],
        [ref[48 + axis * 64 : 112 + axis * 64, :].astype(F32) for axis in range(2)],
    )


def front_scratch(slots):
    return [
        pltpu.VMEM((2, 512, 1024), BF16),
        pltpu.VMEM((512, 1024), BF16),
        pltpu.VMEM((slots * 256, 1024), BF16),
    ]


def front_own_kernel(
    group_ref, offsets_ref, own_ref, row_out, col_out, out_ref, spreads, turned, halves,
):
    def below(ref, part, base, value):
        ref[part * 512 + base : part * 512 + base + 16, :] = value

    lane_table(picked(offsets_ref, 16, 8), 8, 128, 64, col_out, below)
    base = cell_roots()
    small = offset_roots([offsets_ref[4 * index + group_ref[0]] for index in range(4)], 4)
    for index in range(4):
        real, imag = times(row_pick(small, index), base)
        row_out[index * 64 : index * 64 + 64, :] = real.astype(BF16)
        row_out[256 + index * 64 : 320 + index * 64, :] = (-imag).astype(BF16)

    def store(index, facet, value):
        out_ref[facet] = value

    grid_slots([own_ref], row_out, col_out, spreads, turned, halves, store)


def front_own(group, offsets, own):
    return pl.pallas_call(
        front_own_kernel,
        out_shape=[
            jax.ShapeDtypeStruct((512, 512), BF16),
            jax.ShapeDtypeStruct((1024, 1024), BF16),
            jax.ShapeDtypeStruct((32, 64, 128), BF16),
        ],
        in_specs=[smem(), smem(), vmem()],
        out_specs=[vmem()] * 3,
        scratch_shapes=front_scratch(1),
        compiler_params=pltpu.CompilerParams(vmem_limit_bytes=LIMIT),
        cost_estimate=pl.CostEstimate(flops=3 * 10**9, bytes_accessed=4 << 20, transcendentals=0),
        name="front_own",
    )(group, offsets, own)


def front_others_kernel(
    group_ref, first_ref, second_ref, third_ref, row_table, col_table, own_ref, out_ref, spreads, turned, halves,
):
    group = group_ref[0]
    for facet in range(32):
        out_ref[facet, group & 3] = own_ref[facet]

    def store(index, facet, value):
        out_ref[facet, (group + 3 - index) & 3] = value

    grid_slots([first_ref, second_ref, third_ref], row_table, col_table, spreads, turned, halves, store)


def front_others(group, packs, row_table, col_table, own):
    return pl.pallas_call(
        front_others_kernel,
        out_shape=jax.ShapeDtypeStruct((32, 4, 64, 128), BF16),
        in_specs=[smem()] + [vmem()] * 6,
        out_specs=vmem(),
        scratch_shapes=front_scratch(3),
        compiler_params=pltpu.CompilerParams(vmem_limit_bytes=LIMIT),
        cost_estimate=pl.CostEstimate(flops=6 * 10**9, bytes_accessed=4 << 20, transcendentals=0),
        name="front_others",
    )(group, *packs, row_table, col_table, own)


def smem():
    return pl.BlockSpec(memory_space=pltpu.SMEM)


def vmem():
    return pl.BlockSpec(memory_space=pltpu.VMEM)


def hbm():
    return pl.BlockSpec(memory_space=pltpu.HBM)


def tables_kernel(
    layer_ref, offsets_ref, weights_ref, screen_hbm,
    high_out, base_out, small_out, cell_out, own_out, other_out, screen, sems,
):
    layer = layer_ref[0]
    (arrival,) = fetch((screen_hbm.at[0, pl.ds(layer * 256, 256)],), (screen,), sems)
    frequency, _ = lane_steps(picked(offsets_ref, 24, 16), 16, 64)
    high, middle, low = lane_roots(frequency, 0)
    small, cell = offset_roots(picked(offsets_ref, 40, 8), 8), cell_roots()
    for part in range(2):
        high_out[part] = high[part]
        small_out[part] = small[part]
        cell_out[part] = cell[part]
    for index in range(8):
        base = times(row_pick(middle, index), low)
        for part in range(2):
            base_out[part, index * 8 : index * 8 + 8, :] = base[part]
    arrival.wait()
    for side, target in enumerate((own_out, other_out)):
        weight = weights_ref[layer if side == 0 else 1 - layer] * 4.0
        for chunk in range(4):
            rows = slice(chunk * 64, (chunk + 1) * 64)
            turns = screen[rows, :] * weight
            whole = jnp.floor(turns + 0.5)
            cosine, sine = sincos_small((turns - whole) * (0.5 * math.pi))
            real, imag = rotate_quarter(cosine, sine, whole.astype(jnp.int32))
            target[0, rows, :] = real.astype(BF16)
            target[1, rows, :] = imag.astype(BF16)


def tables(layer, offsets, weights, screen):
    return pl.pallas_call(
        tables_kernel,
        out_shape=[
            jax.ShapeDtypeStruct((2, 8, 1024), F32),
            jax.ShapeDtypeStruct((2, 64, 1024), F32),
            jax.ShapeDtypeStruct((2, 8, 512), F32),
            jax.ShapeDtypeStruct((2, 64, 512), F32),
            jax.ShapeDtypeStruct((2, 256, 512), BF16),
            jax.ShapeDtypeStruct((2, 256, 512), BF16),
        ],
        in_specs=[smem(), smem(), smem(), hbm()],
        out_specs=[vmem()] * 6,
        scratch_shapes=[pltpu.VMEM((256, 512), F32), pltpu.SemaphoreType.DMA((1,))],
        compiler_params=pltpu.CompilerParams(vmem_limit_bytes=LIMIT),
        cost_estimate=pl.CostEstimate(flops=10**9, bytes_accessed=8 << 20, transcendentals=0),
        name="tables",
    )(layer, offsets, weights, screen)


def middle_rows(half, blocks, high, base, row_table, store):
    for index in range(4):
        row = pl.ds(half * 4 + index, 1)
        value = times((high[0, row, :], high[1, row, :]), (base[0], base[1]))
        for part in range(2):
            row_table[part * 256 + index * 64 : part * 256 + index * 64 + 64, :] = value[part].astype(BF16)
    sign = jnp.where((iota((1, 128), 1) & 64) == 0, -1.0, 1.0)
    for pair in range(4):
        placed = jnp.concatenate(
            [blocks[pair >> 1, (2 * pair + part) & 3, :].reshape(1024, 128) for part in range(2)], axis=1
        )
        both = dot(row_table[...], placed)
        straight, crossed = both[:256], both[256:]
        for part in range(2):
            lanes = slice(part * 128, part * 128 + 128)
            value = straight[:, lanes] + pltpu.roll(crossed[:, lanes], 64, 1) * sign
            store(slice(pair * 256 + part * 128, pair * 256 + part * 128 + 128), value.astype(BF16))


def screened(middle, col_table, screen):
    facet = dot(middle, col_table)
    return times((facet[:, :512], facet[:, 512:]), (screen[0].astype(F32), screen[1].astype(F32)))


def back_other_kernel(half_ref, blocks, high, base, out_ref, row_table):
    def store(lanes, value):
        out_ref[:, lanes] = value

    middle_rows(half_ref[0], blocks, high, base, row_table, store)


def back_other(half, blocks, high, base):
    return pl.pallas_call(
        back_other_kernel,
        out_shape=jax.ShapeDtypeStruct((256, 1024), BF16),
        in_specs=[smem()] + [vmem()] * 3,
        out_specs=vmem(),
        scratch_shapes=[pltpu.VMEM((512, 1024), BF16)],
        compiler_params=pltpu.CompilerParams(vmem_limit_bytes=LIMIT),
        cost_estimate=pl.CostEstimate(flops=10**9, bytes_accessed=4 << 20, transcendentals=0),
        name="back_other",
    )(half, blocks, high, base)


def back_own_kernel(half_ref, blocks, high, base, small, cell, screen, out_ref, col_out, row_table, middle):
    def store(lanes, value):
        middle[:, lanes] = value

    middle_rows(half_ref[0], blocks, high, base, row_table, store)
    for column in range(8):
        row = slice(column, column + 1)
        value = times((small[0, row, :], small[1, row, :]), (cell[0], cell[1]))
        real, imag = value[0].astype(BF16), value[1].astype(BF16)
        rows = slice(column * 128, column * 128 + 64)
        col_out[rows, :512] = real
        col_out[rows, 512:] = imag
        rows = slice(column * 128 + 64, column * 128 + 128)
        col_out[rows, :512] = -imag
        col_out[rows, 512:] = real
    real, imag = screened(middle[...], col_out[...], screen)
    out_ref[0] = real
    out_ref[1] = imag


def back_own(half, blocks, high, base, small, cell, screen):
    return pl.pallas_call(
        back_own_kernel,
        out_shape=[
            jax.ShapeDtypeStruct((2, 256, 512), F32),
            jax.ShapeDtypeStruct((1024, 1024), BF16),
        ],
        in_specs=[smem()] + [vmem()] * 6,
        out_specs=[vmem(), vmem()],
        scratch_shapes=[pltpu.VMEM((512, 1024), BF16), pltpu.VMEM((256, 1024), BF16)],
        compiler_params=pltpu.CompilerParams(vmem_limit_bytes=LIMIT),
        cost_estimate=pl.CostEstimate(flops=2 * 10**9, bytes_accessed=8 << 20, transcendentals=0),
        name="back_own",
    )(half, blocks, high, base, small, cell, screen)


def finish_kernel(middle_ref, own_ref, col_ref, screen_ref, out_hbm, image, sems):
    leaving = []
    for chunk in range(2):
        lanes = slice(chunk * 256, chunk * 256 + 256)
        facet = [dot(middle_ref[...], col_ref[:, part * 512 + chunk * 256 : part * 512 + chunk * 256 + 256]) for part in range(2)]
        value = times(facet, [screen_ref[part, :, lanes].astype(F32) for part in range(2)])
        for part in range(2):
            image[chunk, part] = own_ref[part, :, lanes] + value[part]
        copy = pltpu.make_async_copy(image.at[chunk], out_hbm.at[:, :, pl.ds(chunk * 256, 256)], sems.at[chunk])
        copy.start()
        leaving.append(copy)
    for copy in leaving:
        copy.wait()


def finish(middle, own, col_table, screen):
    return pl.pallas_call(
        finish_kernel,
        out_shape=jax.ShapeDtypeStruct((2, 256, 512), F32),
        in_specs=[vmem()] * 4,
        out_specs=hbm(),
        scratch_shapes=[pltpu.VMEM((2, 2, 256, 256), F32), pltpu.SemaphoreType.DMA((2,))],
        compiler_params=pltpu.CompilerParams(vmem_limit_bytes=LIMIT),
        cost_estimate=pl.CostEstimate(flops=10**9, bytes_accessed=8 << 20, transcendentals=0),
        name="finish",
    )(middle, own, col_table, screen)


def position(x, z, y):
    return x * 32 + (z % 8) * 4 + y


GROUPS = [
    [position(x, 2 * k + l, y) for l in range(2) for y in range(4) for x in range(4)] for k in range(4)
]


def shifted(turn):
    return [
        (position(x, z, y), position(x, z + 2 * turn, y)) for x in range(4) for z in range(8) for y in range(4)
    ]


def per_device(
    visibilities, kernels, vis_offsets, block_counts,
    sub_rows, sub_cols, facet_rows, facet_cols, screen_n, layer_w,
):
    place = lax.axis_index("sf")
    group = ((place >> 3) & 3).reshape(1)
    own = pack(
        block_counts,
        visibilities.reshape(2, 8, VB), kernels.reshape(2, 8, 8, VB), vis_offsets.reshape(2, 8, VB),
    )
    offsets = jnp.concatenate([facet_rows, facet_cols, sub_rows, sub_cols])
    packs = [lax.ppermute(own, "sf", shifted(turn)) for turn in (1, 2, 3)]
    facet_row_table, facet_col_table, own_sent = front_own(group, offsets, own)
    outgoing = front_others(group, packs, facet_row_table, facet_col_table, own_sent)
    incoming = lax.all_to_all(
        outgoing, "sf", split_axis=0, concat_axis=0, tiled=True, axis_index_groups=GROUPS
    )
    layer = lax.axis_index("wa").reshape(1)
    high, base, small, cell, own_screen, other_screen = tables(layer, offsets, layer_w, screen_n)
    blocks = incoming.reshape(2, 4, 4, 4, CON, 128)
    theirs = back_other(1 - layer, blocks, high, base)
    received = lax.ppermute(theirs, "wa", [(0, 1), (1, 0)])
    own_part, col_table = back_own(layer, blocks, high, base, small, cell, own_screen)
    return finish(received, own_part, col_table, other_screen)[:, None]


def solution(mesh):
    in_specs = (
        P(None, "sf", "wa", None, None),
        P(None, None, "sf", "wa", None, None),
        P(None, "sf", "wa", None, None),
        P("sf", "wa"),
        P(),
        P(),
        P(),
        P(),
        P("sf", None, None),
        P(),
    )
    out_specs = P(None, "sf", "wa", None)
    return jax.shard_map(
        per_device, mesh=mesh, in_specs=in_specs, out_specs=out_specs, check_vma=False
    )
```

```python
import math

import jax
import jax.numpy as jnp
from jax import lax
from jax.experimental import pallas as pl
from jax.experimental.pallas import tpu as pltpu
from jax.sharding import PartitionSpec as P

SUB = 512
CON = 64
FAC = 512
VB = 128
F32 = jnp.float32
BF16 = jnp.bfloat16
NORM = 1.0 / math.sqrt(512.0)
NN = (((1,), (0,)), ((), ()))
NT = (((1,), (1,)), ((), ()))
LIMIT = 20 << 20


def dot(first, second, numbers=NN):
    return lax.dot_general(first, second, numbers, preferred_element_type=F32)


def iota(shape, axis):
    return lax.broadcasted_iota(jnp.int32, shape, axis)


def sincos_small(theta):
    square = theta * theta
    cosine = 1.0 + square * (-0.5 + square * (1.0 / 24 + square * (-1.0 / 720 + square * (1.0 / 40320))))
    sine = theta * (1.0 + square * (-1.0 / 6 + square * (1.0 / 120 + square * (-1.0 / 5040 + square * (1.0 / 362880)))))
    return cosine, sine


def rotate_quarter(cosine, sine, quarter):
    odd = (quarter & 1) == 1
    real = jnp.where(odd, sine, cosine)
    imag = jnp.where(odd, cosine, sine)
    real = jnp.where(((quarter + 1) & 2) == 2, -real, real)
    imag = jnp.where((quarter & 2) == 2, -imag, imag)
    return real, imag


def unit_roots(steps):
    quarter = (steps + 64) >> 7
    rest = steps - (quarter << 7)
    cosine, sine = sincos_small(rest.astype(F32) * (2.0 * math.pi / 512))
    return rotate_quarter(cosine, sine, quarter)


def times(first, second):
    return (
        first[0] * second[0] - first[1] * second[1],
        first[0] * second[1] + first[1] * second[0],
    )


def picked(ref, first, count):
    return [ref[first + index] for index in range(count)]


def cell_roots():
    low = unit_roots(iota((8, 512), 0) * iota((8, 512), 1) & 511)
    high = unit_roots(iota((8, 512), 0) * 8 * iota((8, 512), 1) & 511)
    real, imag = [], []
    for index in range(8):
        row = slice(index, index + 1)
        product = times((high[0][row], high[1][row]), low)
        real.append(product[0])
        imag.append(product[1])
    return jnp.concatenate(real, axis=0), jnp.concatenate(imag, axis=0)


def offset_roots(offsets_ref, count):
    rows = iota((count, 512), 0)
    start = jnp.zeros((count, 512), jnp.int32)
    for index in range(count):
        start = jnp.where(rows == index, offsets_ref[index], start)
    steps = start * iota((count, 512), 1)
    real, imag = unit_roots(steps & 511)
    return real * NORM, imag * NORM


def lane_steps(offsets_ref, count, width):
    shape = (8, count * width)
    lane = iota(shape, 1)
    owner = lane // width
    start = jnp.zeros(shape, jnp.int32)
    for index in range(count):
        start = jnp.where(owner == index, offsets_ref[index], start)
    return start + (lane & 63), lane


def lane_roots(frequency, lead):
    row = iota(frequency.shape, 0)
    high = unit_roots((frequency * row * 64) & 511)
    middle = unit_roots((frequency * row * 8) & 511)
    low = unit_roots((frequency * row + lead) & 511)
    low = (low[0] * NORM, low[1] * NORM)
    return high, middle, low


def row_pick(pair, index):
    return pair[0][index : index + 1], pair[1][index : index + 1]


def fetch(sources, targets, sems):
    copies = [
        pltpu.make_async_copy(source, target, sems.at[index])
        for index, (source, target) in enumerate(zip(sources, targets))
    ]
    for copy in copies:
        copy.start()
    return copies


def pack_kernel(counts, inputs, out_ref):
    live = counts[0, 0]
    slot = iota((8, 128), 0)
    vis = inputs[0:16, :].astype(F32)
    kernels = inputs[16:144, :].astype(F32)
    high = inputs[144:160, :].astype(F32)
    low = inputs[160:176, :].astype(F32)
    samples = [jnp.where(slot < live, vis[part * 8 : part * 8 + 8], 0.0) for part in range(2)]
    out_ref[0:16, :] = jnp.concatenate(samples, axis=0).astype(BF16)
    for axis in range(2):
        rows = slice(axis * 8, axis * 8 + 8)
        digits = jnp.concatenate([high[rows], low[rows]], axis=0)
        out_ref[16 + axis * 16 : 32 + axis * 16, :] = digits.astype(BF16)
        turned = []
        for block in range(8):
            shift = (slot - low[axis * 8 + block : axis * 8 + block + 1, :].astype(jnp.int32)) & 7
            values = jnp.zeros((8, VB), F32)
            for column in range(8):
                row = axis * 64 + column * 8 + block
                values = jnp.where(shift == column, kernels[row : row + 1, :], values)
            turned.append(values)
        out_ref[48 + axis * 64 : 112 + axis * 64, :] = jnp.concatenate(turned, axis=0).astype(BF16)


def pack(counts, vis, kernels, offsets):
    inputs = jnp.concatenate(
        [
            vis.reshape(16, VB), kernels.reshape(128, VB),
            (offsets >> 3).astype(BF16).reshape(16, VB), (offsets & 7).astype(BF16).reshape(16, VB),
        ]
    )
    return pl.pallas_call(
        pack_kernel,
        out_shape=jax.ShapeDtypeStruct((176, 128), BF16),
        in_specs=[smem(), vmem()],
        out_specs=vmem(),
        compiler_params=pltpu.CompilerParams(vmem_limit_bytes=LIMIT),
        name="pack",
    )(counts, inputs)


def lane_table(offsets_ref, count, width, lead, out_ref, place):
    frequency, lane = lane_steps(offsets_ref, count, width)
    high, middle, low = lane_roots(frequency, jnp.where((lane & lead) == 0, 0, 128))
    for index in range(8):
        outer = row_pick(high, index)
        for inner in range(0, 8, 2):
            first = times(times(outer, row_pick(middle, inner)), low)
            second = times(times(outer, row_pick(middle, inner + 1)), low)
            base = index * 64 + inner * 8
            for part in range(2):
                place(out_ref, part, base, jnp.concatenate([first[part], second[part]], axis=0).astype(BF16))


def spread_block(data, axis, block, spread):
    _, digits, kernels = data
    tile = iota((64, 8, 128), 0)
    home = digits[axis][block : block + 1, :] + (
        digits[axis][block + 8 : block + 9, :] > iota((8, 128), 0)
    ).astype(jnp.int32)
    values = kernels[axis][block * 8 : block * 8 + 8, :]
    spread[axis, :, block * VB : (block + 1) * VB] = (
        jnp.where(tile == home[None], values[None], 0.0).reshape(512, VB).astype(BF16)
    )


def turn_rows(data, quarter, row_table, spread, turned):
    samples = data[0]
    lanes = slice(quarter * 256, (quarter + 1) * 256)
    rows = dot(row_table[...], spread[0, :, lanes])
    real_part, imag_part = (
        jnp.concatenate([samples[8 * half + 2 * quarter + part : 8 * half + 2 * quarter + part + 1] for part in range(2)], axis=1)
        for half in range(2)
    )
    real, imag = times((rows[:256], rows[256:]), (real_part, imag_part))
    turned[:256, lanes] = real.astype(BF16)
    turned[256:, lanes] = imag.astype(BF16)


def peer(row, column):
    return (column >> 2) * 16 + (column & 3) * 4 + row * 1


def grid_slots(refs, row_table, col_table, spread, turned, halves, store):
    for index, ref in enumerate(refs):
        data = unpacked(ref)
        for axis in range(2):
            for block in range(8):
                spread_block(data, axis, block, spread)
        for quarter in range(4):
            turn_rows(data, quarter, row_table, spread, turned)
        half = dot(turned[...], spread[1], NT).astype(BF16)
        halves[index * 256 : index * 256 + 256, :512] = half[:256]
        halves[index * 256 : index * 256 + 256, 512:] = half[256:]
    for pair in range(4):
        result = dot(halves[...], col_table[:, pair * 256 : pair * 256 + 256]).astype(BF16)
        for index in range(len(refs)):
            for row in range(4):
                for part in range(2):
                    start = index * 256 + row * 64
                    value = result[start : start + 64, part * 128 : (part + 1) * 128]
                    store(index, peer(row, 2 * pair + part), value)


def unpacked(ref):
    return (
        ref[0:16, :].astype(F32),
        [ref[16 + axis * 16 : 32 + axis * 16, :].astype(jnp.int32) for axis in range(2)],
        [ref[48 + axis * 64 : 112 + axis * 64, :].astype(F32) for axis in range(2)],
    )


def front_scratch(slots):
    return [
        pltpu.VMEM((2, 512, 1024), BF16),
        pltpu.VMEM((512, 1024), BF16),
        pltpu.VMEM((slots * 256, 1024), BF16),
    ]


def front_own_kernel(
    group_ref, offsets_ref, own_ref, row_out, col_out, out_ref, spreads, turned, halves,
):
    def below(ref, part, base, value):
        ref[part * 512 + base : part * 512 + base + 16, :] = value

    lane_table(picked(offsets_ref, 16, 8), 8, 128, 64, col_out, below)
    base = cell_roots()
    small = offset_roots([offsets_ref[4 * index + group_ref[0]] for index in range(4)], 4)
    for index in range(4):
        real, imag = times(row_pick(small, index), base)
        row_out[index * 64 : index * 64 + 64, :] = real.astype(BF16)
        row_out[256 + index * 64 : 320 + index * 64, :] = (-imag).astype(BF16)

    def store(index, facet, value):
        out_ref[facet] = value

    grid_slots([own_ref], row_out, col_out, spreads, turned, halves, store)


def front_own(group, offsets, own):
    return pl.pallas_call(
        front_own_kernel,
        out_shape=[
            jax.ShapeDtypeStruct((512, 512), BF16),
            jax.ShapeDtypeStruct((1024, 1024), BF16),
            jax.ShapeDtypeStruct((32, 64, 128), BF16),
        ],
        in_specs=[smem(), smem(), vmem()],
        out_specs=[vmem()] * 3,
        scratch_shapes=front_scratch(1),
        compiler_params=pltpu.CompilerParams(vmem_limit_bytes=LIMIT),
        cost_estimate=pl.CostEstimate(flops=3 * 10**9, bytes_accessed=4 << 20, transcendentals=0),
        name="front_own",
    )(group, offsets, own)


def front_others_kernel(
    group_ref, first_ref, second_ref, third_ref, row_table, col_table, own_ref, out_ref, spreads, turned, halves,
):
    group = group_ref[0]
    for facet in range(32):
        out_ref[facet, group & 3] = own_ref[facet]

    def store(index, facet, value):
        out_ref[facet, (group + 3 - index) & 3] = value

    grid_slots([first_ref, second_ref, third_ref], row_table, col_table, spreads, turned, halves, store)


def front_others(group, packs, row_table, col_table, own):
    return pl.pallas_call(
        front_others_kernel,
        out_shape=jax.ShapeDtypeStruct((32, 4, 64, 128), BF16),
        in_specs=[smem()] + [vmem()] * 6,
        out_specs=vmem(),
        scratch_shapes=front_scratch(3),
        compiler_params=pltpu.CompilerParams(vmem_limit_bytes=LIMIT),
        cost_estimate=pl.CostEstimate(flops=6 * 10**9, bytes_accessed=4 << 20, transcendentals=0),
        name="front_others",
    )(group, *packs, row_table, col_table, own)


def smem():
    return pl.BlockSpec(memory_space=pltpu.SMEM)


def vmem():
    return pl.BlockSpec(memory_space=pltpu.VMEM)


def hbm():
    return pl.BlockSpec(memory_space=pltpu.HBM)


def tables_kernel(
    layer_ref, offsets_ref, weights_ref, screen_hbm,
    high_out, base_out, small_out, cell_out, own_out, other_out, screen, sems,
):
    layer = layer_ref[0]
    (arrival,) = fetch((screen_hbm.at[0, pl.ds(layer * 256, 256)],), (screen,), sems)
    frequency, _ = lane_steps(picked(offsets_ref, 24, 16), 16, 64)
    high, middle, low = lane_roots(frequency, 0)
    small, cell = offset_roots(picked(offsets_ref, 40, 8), 8), cell_roots()
    for part in range(2):
        high_out[part] = high[part]
        small_out[part] = small[part]
        cell_out[part] = cell[part]
    for index in range(8):
        base = times(row_pick(middle, index), low)
        for part in range(2):
            base_out[part, index * 8 : index * 8 + 8, :] = base[part]
    arrival.wait()
    for side, target in enumerate((own_out, other_out)):
        weight = weights_ref[layer if side == 0 else 1 - layer] * 4.0
        for chunk in range(4):
            rows = slice(chunk * 64, (chunk + 1) * 64)
            turns = screen[rows, :] * weight
            whole = jnp.floor(turns + 0.5)
            cosine, sine = sincos_small((turns - whole) * (0.5 * math.pi))
            real, imag = rotate_quarter(cosine, sine, whole.astype(jnp.int32))
            target[0, rows, :] = real.astype(BF16)
            target[1, rows, :] = imag.astype(BF16)


def tables(layer, offsets, weights, screen):
    return pl.pallas_call(
        tables_kernel,
        out_shape=[
            jax.ShapeDtypeStruct((2, 8, 1024), F32),
            jax.ShapeDtypeStruct((2, 64, 1024), F32),
            jax.ShapeDtypeStruct((2, 8, 512), F32),
            jax.ShapeDtypeStruct((2, 64, 512), F32),
            jax.ShapeDtypeStruct((2, 256, 512), BF16),
            jax.ShapeDtypeStruct((2, 256, 512), BF16),
        ],
        in_specs=[smem(), smem(), smem(), hbm()],
        out_specs=[vmem()] * 6,
        scratch_shapes=[pltpu.VMEM((256, 512), F32), pltpu.SemaphoreType.DMA((1,))],
        compiler_params=pltpu.CompilerParams(vmem_limit_bytes=LIMIT),
        cost_estimate=pl.CostEstimate(flops=10**9, bytes_accessed=8 << 20, transcendentals=0),
        name="tables",
    )(layer, offsets, weights, screen)


def middle_rows(half, blocks, high, base, row_table, store):
    for index in range(4):
        row = pl.ds(half * 4 + index, 1)
        value = times((high[0, row, :], high[1, row, :]), (base[0], base[1]))
        for part in range(2):
            row_table[part * 256 + index * 64 : part * 256 + index * 64 + 64, :] = value[part].astype(BF16)
    sign = jnp.where((iota((1, 128), 1) & 64) == 0, -1.0, 1.0)
    for pair in range(4):
        placed = jnp.concatenate(
            [blocks[pair >> 1, (2 * pair + part) & 3, :].reshape(1024, 128) for part in range(2)], axis=1
        )
        both = dot(row_table[...], placed)
        straight, crossed = both[:256], both[256:]
        for part in range(2):
            lanes = slice(part * 128, part * 128 + 128)
            value = straight[:, lanes] + pltpu.roll(crossed[:, lanes], 64, 1) * sign
            store(slice(pair * 256 + part * 128, pair * 256 + part * 128 + 128), value.astype(BF16))


def screened(middle, col_table, screen):
    facet = dot(middle, col_table)
    return times((facet[:, :512], facet[:, 512:]), (screen[0].astype(F32), screen[1].astype(F32)))


def back_other_kernel(half_ref, blocks, high, base, out_ref, row_table):
    def store(lanes, value):
        out_ref[:, lanes] = value

    middle_rows(half_ref[0], blocks, high, base, row_table, store)


def back_other(half, blocks, high, base):
    return pl.pallas_call(
        back_other_kernel,
        out_shape=jax.ShapeDtypeStruct((256, 1024), BF16),
        in_specs=[smem()] + [vmem()] * 3,
        out_specs=vmem(),
        scratch_shapes=[pltpu.VMEM((512, 1024), BF16)],
        compiler_params=pltpu.CompilerParams(vmem_limit_bytes=LIMIT),
        cost_estimate=pl.CostEstimate(flops=10**9, bytes_accessed=4 << 20, transcendentals=0),
        name="back_other",
    )(half, blocks, high, base)


def back_own_kernel(half_ref, blocks, high, base, small, cell, screen, out_ref, col_out, row_table, middle):
    def store(lanes, value):
        middle[:, lanes] = value

    middle_rows(half_ref[0], blocks, high, base, row_table, store)
    for column in range(8):
        row = slice(column, column + 1)
        value = times((small[0, row, :], small[1, row, :]), (cell[0], cell[1]))
        real, imag = value[0].astype(BF16), value[1].astype(BF16)
        rows = slice(column * 128, column * 128 + 64)
        col_out[rows, :512] = real
        col_out[rows, 512:] = imag
        rows = slice(column * 128 + 64, column * 128 + 128)
        col_out[rows, :512] = -imag
        col_out[rows, 512:] = real
    real, imag = screened(middle[...], col_out[...], screen)
    out_ref[0] = real
    out_ref[1] = imag


def back_own(half, blocks, high, base, small, cell, screen):
    return pl.pallas_call(
        back_own_kernel,
        out_shape=[
            jax.ShapeDtypeStruct((2, 256, 512), F32),
            jax.ShapeDtypeStruct((1024, 1024), BF16),
        ],
        in_specs=[smem()] + [vmem()] * 6,
        out_specs=[vmem(), vmem()],
        scratch_shapes=[pltpu.VMEM((512, 1024), BF16), pltpu.VMEM((256, 1024), BF16)],
        compiler_params=pltpu.CompilerParams(vmem_limit_bytes=LIMIT),
        cost_estimate=pl.CostEstimate(flops=2 * 10**9, bytes_accessed=8 << 20, transcendentals=0),
        name="back_own",
    )(half, blocks, high, base, small, cell, screen)


def finish_kernel(middle_ref, own_ref, col_ref, screen_ref, out_hbm, image, sems):
    leaving = []
    for chunk in range(2):
        lanes = slice(chunk * 256, chunk * 256 + 256)
        facet = [dot(middle_ref[...], col_ref[:, part * 512 + chunk * 256 : part * 512 + chunk * 256 + 256]) for part in range(2)]
        value = times(facet, [screen_ref[part, :, lanes].astype(F32) for part in range(2)])
        for part in range(2):
            image[chunk, part] = own_ref[part, :, lanes] + value[part]
        copy = pltpu.make_async_copy(image.at[chunk], out_hbm.at[:, :, pl.ds(chunk * 256, 256)], sems.at[chunk])
        copy.start()
        leaving.append(copy)
    for copy in leaving:
        copy.wait()


def finish(middle, own, col_table, screen):
    return pl.pallas_call(
        finish_kernel,
        out_shape=jax.ShapeDtypeStruct((2, 256, 512), F32),
        in_specs=[vmem()] * 4,
        out_specs=hbm(),
        scratch_shapes=[pltpu.VMEM((2, 2, 256, 256), F32), pltpu.SemaphoreType.DMA((2,))],
        compiler_params=pltpu.CompilerParams(vmem_limit_bytes=LIMIT),
        cost_estimate=pl.CostEstimate(flops=10**9, bytes_accessed=8 << 20, transcendentals=0),
        name="finish",
    )(middle, own, col_table, screen)


def position(x, z, y):
    return x * 32 + (z % 8) * 4 + y


GROUPS = [
    [position(x, 2 * k + l, y) for l in range(2) for y in range(4) for x in range(4)] for k in range(4)
]


def shifted(turn):
    return [
        (position(x, z, y), position(x, z + 2 * turn, y)) for x in range(4) for z in range(8) for y in range(4)
    ]


def per_device(
    visibilities, kernels, vis_offsets, block_counts,
    sub_rows, sub_cols, facet_rows, facet_cols, screen_n, layer_w,
):
    place = lax.axis_index("sf")
    group = ((place >> 3) & 3).reshape(1)
    own = pack(
        block_counts,
        visibilities.reshape(2, 8, VB), kernels.reshape(2, 8, 8, VB), vis_offsets.reshape(2, 8, VB),
    )
    offsets = jnp.concatenate([facet_rows, facet_cols, sub_rows, sub_cols])
    first, third = (lax.ppermute(own, "sf", shifted(turn)) for turn in (1, 3))
    packs = [first, lax.ppermute(first, "sf", shifted(1)), third]
    facet_row_table, facet_col_table, own_sent = front_own(group, offsets, own)
    outgoing = front_others(group, packs, facet_row_table, facet_col_table, own_sent)
    incoming = lax.all_to_all(
        outgoing, "sf", split_axis=0, concat_axis=0, tiled=True, axis_index_groups=GROUPS
    )
    layer = lax.axis_index("wa").reshape(1)
    high, base, small, cell, own_screen, other_screen = tables(layer, offsets, layer_w, screen_n)
    blocks = incoming.reshape(2, 4, 4, 4, CON, 128)
    theirs = back_other(1 - layer, blocks, high, base)
    received = lax.ppermute(theirs, "wa", [(0, 1), (1, 0)])
    own_part, col_table = back_own(layer, blocks, high, base, small, cell, own_screen)
    return finish(received, own_part, col_table, other_screen)[:, None]


def solution(mesh):
    in_specs = (
        P(None, "sf", "wa", None, None),
        P(None, None, "sf", "wa", None, None),
        P(None, "sf", "wa", None, None),
        P("sf", "wa"),
        P(),
        P(),
        P(),
        P(),
        P("sf", None, None),
        P(),
    )
    out_specs = P(None, "sf", "wa", None)
    return jax.shard_map(
        per_device, mesh=mesh, in_specs=in_specs, out_specs=out_specs, check_vma=False
    )
```

```python
import math

import jax
import jax.numpy as jnp
from jax import lax
from jax.experimental import pallas as pl
from jax.experimental.pallas import tpu as pltpu
from jax.sharding import PartitionSpec as P

SUB = 512
CON = 64
FAC = 512
VB = 128
F32 = jnp.float32
BF16 = jnp.bfloat16
NORM = 1.0 / math.sqrt(512.0)
NN = (((1,), (0,)), ((), ()))
NT = (((1,), (1,)), ((), ()))
LIMIT = 20 << 20


def dot(first, second, numbers=NN):
    return lax.dot_general(first, second, numbers, preferred_element_type=F32)


def iota(shape, axis):
    return lax.broadcasted_iota(jnp.int32, shape, axis)


def sincos_small(theta):
    square = theta * theta
    cosine = 1.0 + square * (-0.5 + square * (1.0 / 24 + square * (-1.0 / 720 + square * (1.0 / 40320))))
    sine = theta * (1.0 + square * (-1.0 / 6 + square * (1.0 / 120 + square * (-1.0 / 5040 + square * (1.0 / 362880)))))
    return cosine, sine


def rotate_quarter(cosine, sine, quarter):
    odd = (quarter & 1) == 1
    real = jnp.where(odd, sine, cosine)
    imag = jnp.where(odd, cosine, sine)
    real = jnp.where(((quarter + 1) & 2) == 2, -real, real)
    imag = jnp.where((quarter & 2) == 2, -imag, imag)
    return real, imag


def unit_roots(steps):
    quarter = (steps + 64) >> 7
    rest = steps - (quarter << 7)
    cosine, sine = sincos_small(rest.astype(F32) * (2.0 * math.pi / 512))
    return rotate_quarter(cosine, sine, quarter)


def times(first, second):
    return (
        first[0] * second[0] - first[1] * second[1],
        first[0] * second[1] + first[1] * second[0],
    )


def picked(ref, first, count):
    return [ref[first + index] for index in range(count)]


def cell_roots():
    low = unit_roots(iota((8, 512), 0) * iota((8, 512), 1) & 511)
    high = unit_roots(iota((8, 512), 0) * 8 * iota((8, 512), 1) & 511)
    real, imag = [], []
    for index in range(8):
        row = slice(index, index + 1)
        product = times((high[0][row], high[1][row]), low)
        real.append(product[0])
        imag.append(product[1])
    return jnp.concatenate(real, axis=0), jnp.concatenate(imag, axis=0)


def offset_roots(offsets_ref, count):
    rows = iota((count, 512), 0)
    start = jnp.zeros((count, 512), jnp.int32)
    for index in range(count):
        start = jnp.where(rows == index, offsets_ref[index], start)
    steps = start * iota((count, 512), 1)
    real, imag = unit_roots(steps & 511)
    return real * NORM, imag * NORM


def lane_steps(offsets_ref, count, width):
    shape = (8, count * width)
    lane = iota(shape, 1)
    owner = lane // width
    start = jnp.zeros(shape, jnp.int32)
    for index in range(count):
        start = jnp.where(owner == index, offsets_ref[index], start)
    return start + (lane & 63), lane


def lane_roots(frequency, lead):
    row = iota(frequency.shape, 0)
    high = unit_roots((frequency * row * 64) & 511)
    middle = unit_roots((frequency * row * 8) & 511)
    low = unit_roots((frequency * row + lead) & 511)
    low = (low[0] * NORM, low[1] * NORM)
    return high, middle, low


def row_pick(pair, index):
    return pair[0][index : index + 1], pair[1][index : index + 1]


def fetch(sources, targets, sems):
    copies = [
        pltpu.make_async_copy(source, target, sems.at[index])
        for index, (source, target) in enumerate(zip(sources, targets))
    ]
    for copy in copies:
        copy.start()
    return copies


def pack_kernel(counts, inputs, out_ref):
    live = counts[0, 0]
    slot = iota((8, 128), 0)
    vis = inputs[0:16, :].astype(F32)
    kernels = inputs[16:144, :].astype(F32)
    high = inputs[144:160, :].astype(F32)
    low = inputs[160:176, :].astype(F32)
    samples = [jnp.where(slot < live, vis[part * 8 : part * 8 + 8], 0.0) for part in range(2)]
    out_ref[0:16, :] = jnp.concatenate(samples, axis=0).astype(BF16)
    for axis in range(2):
        rows = slice(axis * 8, axis * 8 + 8)
        digits = jnp.concatenate([high[rows], low[rows]], axis=0)
        out_ref[16 + axis * 16 : 32 + axis * 16, :] = digits.astype(BF16)
        turned = []
        for block in range(8):
            shift = (slot - low[axis * 8 + block : axis * 8 + block + 1, :].astype(jnp.int32)) & 7
            values = jnp.zeros((8, VB), F32)
            for column in range(8):
                row = axis * 64 + column * 8 + block
                values = jnp.where(shift == column, kernels[row : row + 1, :], values)
            turned.append(values)
        out_ref[48 + axis * 64 : 112 + axis * 64, :] = jnp.concatenate(turned, axis=0).astype(BF16)


def pack(counts, vis, kernels, offsets):
    inputs = jnp.concatenate(
        [
            vis.reshape(16, VB), kernels.reshape(128, VB),
            (offsets >> 3).astype(BF16).reshape(16, VB), (offsets & 7).astype(BF16).reshape(16, VB),
        ]
    )
    return pl.pallas_call(
        pack_kernel,
        out_shape=jax.ShapeDtypeStruct((176, 128), BF16),
        in_specs=[smem(), vmem()],
        out_specs=vmem(),
        compiler_params=pltpu.CompilerParams(vmem_limit_bytes=LIMIT),
        name="pack",
    )(counts, inputs)


def lane_table(offsets_ref, count, width, lead, out_ref, place):
    frequency, lane = lane_steps(offsets_ref, count, width)
    high, middle, low = lane_roots(frequency, jnp.where((lane & lead) == 0, 0, 128))
    for index in range(8):
        outer = row_pick(high, index)
        for inner in range(0, 8, 2):
            first = times(times(outer, row_pick(middle, inner)), low)
            second = times(times(outer, row_pick(middle, inner + 1)), low)
            base = index * 64 + inner * 8
            for part in range(2):
                place(out_ref, part, base, jnp.concatenate([first[part], second[part]], axis=0).astype(BF16))


def spread_block(data, axis, block, spread):
    _, digits, kernels = data
    tile = iota((64, 8, 128), 0)
    home = digits[axis][block : block + 1, :] + (
        digits[axis][block + 8 : block + 9, :] > iota((8, 128), 0)
    ).astype(jnp.int32)
    values = kernels[axis][block * 8 : block * 8 + 8, :]
    spread[axis, :, block * VB : (block + 1) * VB] = (
        jnp.where(tile == home[None], values[None], 0.0).reshape(512, VB).astype(BF16)
    )


def turn_rows(data, quarter, row_table, spread, turned):
    samples = data[0]
    lanes = slice(quarter * 256, (quarter + 1) * 256)
    rows = dot(row_table[...], spread[0, :, lanes])
    real_part, imag_part = (
        jnp.concatenate([samples[8 * half + 2 * quarter + part : 8 * half + 2 * quarter + part + 1] for part in range(2)], axis=1)
        for half in range(2)
    )
    real, imag = times((rows[:256], rows[256:]), (real_part, imag_part))
    turned[:256, lanes] = real.astype(BF16)
    turned[256:, lanes] = imag.astype(BF16)


def peer(row, column):
    return (column >> 2) * 16 + row * 4 + (column & 3) * 1


def grid_slots(refs, row_table, col_table, spread, turned, halves, store):
    for index, ref in enumerate(refs):
        data = unpacked(ref)
        for axis in range(2):
            for block in range(8):
                spread_block(data, axis, block, spread)
        for quarter in range(4):
            turn_rows(data, quarter, row_table, spread, turned)
        half = dot(turned[...], spread[1], NT).astype(BF16)
        halves[index * 256 : index * 256 + 256, :512] = half[:256]
        halves[index * 256 : index * 256 + 256, 512:] = half[256:]
    for pair in range(4):
        result = dot(halves[...], col_table[:, pair * 256 : pair * 256 + 256]).astype(BF16)
        for index in range(len(refs)):
            for row in range(4):
                for part in range(2):
                    start = index * 256 + row * 64
                    value = result[start : start + 64, part * 128 : (part + 1) * 128]
                    store(index, peer(row, 2 * pair + part), value)


def unpacked(ref):
    return (
        ref[0:16, :].astype(F32),
        [ref[16 + axis * 16 : 32 + axis * 16, :].astype(jnp.int32) for axis in range(2)],
        [ref[48 + axis * 64 : 112 + axis * 64, :].astype(F32) for axis in range(2)],
    )


def front_scratch(slots):
    return [
        pltpu.VMEM((2, 512, 1024), BF16),
        pltpu.VMEM((512, 1024), BF16),
        pltpu.VMEM((slots * 256, 1024), BF16),
    ]


def front_own_kernel(
    group_ref, offsets_ref, own_ref, row_out, col_out, out_ref, spreads, turned, halves,
):
    def below(ref, part, base, value):
        ref[part * 512 + base : part * 512 + base + 16, :] = value

    lane_table(picked(offsets_ref, 16, 8), 8, 128, 64, col_out, below)
    base = cell_roots()
    small = offset_roots([offsets_ref[4 * index + group_ref[0]] for index in range(4)], 4)
    for index in range(4):
        real, imag = times(row_pick(small, index), base)
        row_out[index * 64 : index * 64 + 64, :] = real.astype(BF16)
        row_out[256 + index * 64 : 320 + index * 64, :] = (-imag).astype(BF16)

    def store(index, facet, value):
        out_ref[facet] = value

    grid_slots([own_ref], row_out, col_out, spreads, turned, halves, store)


def front_own(group, offsets, own):
    return pl.pallas_call(
        front_own_kernel,
        out_shape=[
            jax.ShapeDtypeStruct((512, 512), BF16),
            jax.ShapeDtypeStruct((1024, 1024), BF16),
            jax.ShapeDtypeStruct((32, 64, 128), BF16),
        ],
        in_specs=[smem(), smem(), vmem()],
        out_specs=[vmem()] * 3,
        scratch_shapes=front_scratch(1),
        compiler_params=pltpu.CompilerParams(vmem_limit_bytes=LIMIT),
        cost_estimate=pl.CostEstimate(flops=3 * 10**9, bytes_accessed=4 << 20, transcendentals=0),
        name="front_own",
    )(group, offsets, own)


def front_others_kernel(
    group_ref, first_ref, second_ref, third_ref, row_table, col_table, own_ref, out_ref, spreads, turned, halves,
):
    group = group_ref[0]
    for facet in range(32):
        out_ref[facet, group & 3] = own_ref[facet]

    def store(index, facet, value):
        out_ref[facet, (group + 3 - index) & 3] = value

    grid_slots([first_ref, second_ref, third_ref], row_table, col_table, spreads, turned, halves, store)


def front_others(group, packs, row_table, col_table, own):
    return pl.pallas_call(
        front_others_kernel,
        out_shape=jax.ShapeDtypeStruct((32, 4, 64, 128), BF16),
        in_specs=[smem()] + [vmem()] * 6,
        out_specs=vmem(),
        scratch_shapes=front_scratch(3),
        compiler_params=pltpu.CompilerParams(vmem_limit_bytes=LIMIT),
        cost_estimate=pl.CostEstimate(flops=6 * 10**9, bytes_accessed=4 << 20, transcendentals=0),
        name="front_others",
    )(group, *packs, row_table, col_table, own)


def smem():
    return pl.BlockSpec(memory_space=pltpu.SMEM)


def vmem():
    return pl.BlockSpec(memory_space=pltpu.VMEM)


def hbm():
    return pl.BlockSpec(memory_space=pltpu.HBM)


def tables_kernel(
    layer_ref, offsets_ref, weights_ref, screen_hbm,
    high_out, base_out, small_out, cell_out, own_out, other_out, screen, sems,
):
    layer = layer_ref[0]
    (arrival,) = fetch((screen_hbm.at[0, pl.ds(layer * 256, 256)],), (screen,), sems)
    frequency, _ = lane_steps(picked(offsets_ref, 24, 16), 16, 64)
    high, middle, low = lane_roots(frequency, 0)
    small, cell = offset_roots(picked(offsets_ref, 40, 8), 8), cell_roots()
    for part in range(2):
        high_out[part] = high[part]
        small_out[part] = small[part]
        cell_out[part] = cell[part]
    for index in range(8):
        base = times(row_pick(middle, index), low)
        for part in range(2):
            base_out[part, index * 8 : index * 8 + 8, :] = base[part]
    arrival.wait()
    for side, target in enumerate((own_out, other_out)):
        weight = weights_ref[layer if side == 0 else 1 - layer] * 4.0
        for chunk in range(4):
            rows = slice(chunk * 64, (chunk + 1) * 64)
            turns = screen[rows, :] * weight
            whole = jnp.floor(turns + 0.5)
            cosine, sine = sincos_small((turns - whole) * (0.5 * math.pi))
            real, imag = rotate_quarter(cosine, sine, whole.astype(jnp.int32))
            target[0, rows, :] = real.astype(BF16)
            target[1, rows, :] = imag.astype(BF16)


def tables(layer, offsets, weights, screen):
    return pl.pallas_call(
        tables_kernel,
        out_shape=[
            jax.ShapeDtypeStruct((2, 8, 1024), F32),
            jax.ShapeDtypeStruct((2, 64, 1024), F32),
            jax.ShapeDtypeStruct((2, 8, 512), F32),
            jax.ShapeDtypeStruct((2, 64, 512), F32),
            jax.ShapeDtypeStruct((2, 256, 512), BF16),
            jax.ShapeDtypeStruct((2, 256, 512), BF16),
        ],
        in_specs=[smem(), smem(), smem(), hbm()],
        out_specs=[vmem()] * 6,
        scratch_shapes=[pltpu.VMEM((256, 512), F32), pltpu.SemaphoreType.DMA((1,))],
        compiler_params=pltpu.CompilerParams(vmem_limit_bytes=LIMIT),
        cost_estimate=pl.CostEstimate(flops=10**9, bytes_accessed=8 << 20, transcendentals=0),
        name="tables",
    )(layer, offsets, weights, screen)


def middle_rows(half, blocks, high, base, row_table, store):
    for index in range(4):
        row = pl.ds(half * 4 + index, 1)
        value = times((high[0, row, :], high[1, row, :]), (base[0], base[1]))
        for part in range(2):
            row_table[part * 256 + index * 64 : part * 256 + index * 64 + 64, :] = value[part].astype(BF16)
    sign = jnp.where((iota((1, 128), 1) & 64) == 0, -1.0, 1.0)
    for pair in range(4):
        placed = jnp.concatenate(
            [blocks[pair >> 1, :, (2 * pair + part) & 3].reshape(1024, 128) for part in range(2)], axis=1
        )
        both = dot(row_table[...], placed)
        straight, crossed = both[:256], both[256:]
        for part in range(2):
            lanes = slice(part * 128, part * 128 + 128)
            value = straight[:, lanes] + pltpu.roll(crossed[:, lanes], 64, 1) * sign
            store(slice(pair * 256 + part * 128, pair * 256 + part * 128 + 128), value.astype(BF16))


def screened(middle, col_table, screen):
    facet = dot(middle, col_table)
    return times((facet[:, :512], facet[:, 512:]), (screen[0].astype(F32), screen[1].astype(F32)))


def back_other_kernel(half_ref, blocks, high, base, out_ref, row_table):
    def store(lanes, value):
        out_ref[:, lanes] = value

    middle_rows(half_ref[0], blocks, high, base, row_table, store)


def back_other(half, blocks, high, base):
    return pl.pallas_call(
        back_other_kernel,
        out_shape=jax.ShapeDtypeStruct((256, 1024), BF16),
        in_specs=[smem()] + [vmem()] * 3,
        out_specs=vmem(),
        scratch_shapes=[pltpu.VMEM((512, 1024), BF16)],
        compiler_params=pltpu.CompilerParams(vmem_limit_bytes=LIMIT),
        cost_estimate=pl.CostEstimate(flops=10**9, bytes_accessed=4 << 20, transcendentals=0),
        name="back_other",
    )(half, blocks, high, base)


def back_own_kernel(half_ref, blocks, high, base, small, cell, screen, out_ref, col_out, row_table, middle):
    def store(lanes, value):
        middle[:, lanes] = value

    middle_rows(half_ref[0], blocks, high, base, row_table, store)
    for column in range(8):
        row = slice(column, column + 1)
        value = times((small[0, row, :], small[1, row, :]), (cell[0], cell[1]))
        real, imag = value[0].astype(BF16), value[1].astype(BF16)
        rows = slice(column * 128, column * 128 + 64)
        col_out[rows, :512] = real
        col_out[rows, 512:] = imag
        rows = slice(column * 128 + 64, column * 128 + 128)
        col_out[rows, :512] = -imag
        col_out[rows, 512:] = real
    real, imag = screened(middle[...], col_out[...], screen)
    out_ref[0] = real
    out_ref[1] = imag


def back_own(half, blocks, high, base, small, cell, screen):
    return pl.pallas_call(
        back_own_kernel,
        out_shape=[
            jax.ShapeDtypeStruct((2, 256, 512), F32),
            jax.ShapeDtypeStruct((1024, 1024), BF16),
        ],
        in_specs=[smem()] + [vmem()] * 6,
        out_specs=[vmem(), vmem()],
        scratch_shapes=[pltpu.VMEM((512, 1024), BF16), pltpu.VMEM((256, 1024), BF16)],
        compiler_params=pltpu.CompilerParams(vmem_limit_bytes=LIMIT),
        cost_estimate=pl.CostEstimate(flops=2 * 10**9, bytes_accessed=8 << 20, transcendentals=0),
        name="back_own",
    )(half, blocks, high, base, small, cell, screen)


def finish_kernel(middle_ref, own_ref, col_ref, screen_ref, out_hbm, image, sems):
    leaving = []
    for chunk in range(2):
        lanes = slice(chunk * 256, chunk * 256 + 256)
        facet = [dot(middle_ref[...], col_ref[:, part * 512 + chunk * 256 : part * 512 + chunk * 256 + 256]) for part in range(2)]
        value = times(facet, [screen_ref[part, :, lanes].astype(F32) for part in range(2)])
        for part in range(2):
            image[chunk, part] = own_ref[part, :, lanes] + value[part]
        copy = pltpu.make_async_copy(image.at[chunk], out_hbm.at[:, :, pl.ds(chunk * 256, 256)], sems.at[chunk])
        copy.start()
        leaving.append(copy)
    for copy in leaving:
        copy.wait()


def finish(middle, own, col_table, screen):
    return pl.pallas_call(
        finish_kernel,
        out_shape=jax.ShapeDtypeStruct((2, 256, 512), F32),
        in_specs=[vmem()] * 4,
        out_specs=hbm(),
        scratch_shapes=[pltpu.VMEM((2, 2, 256, 256), F32), pltpu.SemaphoreType.DMA((2,))],
        compiler_params=pltpu.CompilerParams(vmem_limit_bytes=LIMIT),
        cost_estimate=pl.CostEstimate(flops=10**9, bytes_accessed=8 << 20, transcendentals=0),
        name="finish",
    )(middle, own, col_table, screen)


def position(x, z, y):
    return x * 32 + (z % 8) * 4 + y


GROUPS = [
    [position(x, 2 * k + l, y) for l in range(2) for x in range(4) for y in range(4)] for k in range(4)
]


def shifted(turn):
    return [
        (position(x, z, y), position(x, z + 2 * turn, y)) for x in range(4) for z in range(8) for y in range(4)
    ]


def per_device(
    visibilities, kernels, vis_offsets, block_counts,
    sub_rows, sub_cols, facet_rows, facet_cols, screen_n, layer_w,
):
    place = lax.axis_index("sf")
    group = ((place >> 3) & 3).reshape(1)
    own = pack(
        block_counts,
        visibilities.reshape(2, 8, VB), kernels.reshape(2, 8, 8, VB), vis_offsets.reshape(2, 8, VB),
    )
    offsets = jnp.concatenate([facet_rows, facet_cols, sub_rows, sub_cols])
    first, third = (lax.ppermute(own, "sf", shifted(turn)) for turn in (1, 3))
    packs = [first, lax.ppermute(first, "sf", shifted(1)), third]
    facet_row_table, facet_col_table, own_sent = front_own(group, offsets, own)
    outgoing = front_others(group, packs, facet_row_table, facet_col_table, own_sent)
    incoming = lax.all_to_all(
        outgoing, "sf", split_axis=0, concat_axis=0, tiled=True, axis_index_groups=GROUPS
    )
    layer = lax.axis_index("wa").reshape(1)
    high, base, small, cell, own_screen, other_screen = tables(layer, offsets, layer_w, screen_n)
    blocks = incoming.reshape(2, 4, 4, 4, CON, 128)
    theirs = back_other(1 - layer, blocks, high, base)
    received = lax.ppermute(theirs, "wa", [(0, 1), (1, 0)])
    own_part, col_table = back_own(layer, blocks, high, base, small, cell, own_screen)
    return finish(received, own_part, col_table, other_screen)[:, None]


def solution(mesh):
    in_specs = (
        P(None, "sf", "wa", None, None),
        P(None, None, "sf", "wa", None, None),
        P(None, "sf", "wa", None, None),
        P("sf", "wa"),
        P(),
        P(),
        P(),
        P(),
        P("sf", None, None),
        P(),
    )
    out_specs = P(None, "sf", "wa", None)
    return jax.shard_map(
        per_device, mesh=mesh, in_specs=in_specs, out_specs=out_specs, check_vma=False
    )
```
